512 devices in a mesh: dp: 16 (over z, core), expert: 8 (over y), mp: 4 (over x).
Axes of the slice: x: 4, y: 8, z: 8, core: 2. Of those that a mesh axis runs over, the one named last changes fastest.
Arguments:
- tokens: bfloat16 [16384, 2048], P(('dp', 'expert')), may hold values from -6 to 6
- out_grad: bfloat16 [16384, 2048], P(('dp', 'expert')), may hold values from -1.5 to 1.5
- routes: int32 [16384, 2], P(('dp', 'expert')), may hold values from 0 to 7, as said below
- gate_values: float32 [16384, 2], P(('dp', 'expert')), may hold values from 0.2 to 1
- gate_proj: bfloat16 [8, 704, 2048], P('expert', 'mp', 'dp'), may hold values from -0.125 to 0.125
- up_proj: bfloat16 [8, 704, 2048], P('expert', 'mp', 'dp'), may hold values from -0.125 to 0.125
- down_proj: bfloat16 [8, 704, 2048], P('expert', 'mp', 'dp'), may hold values from -0.21875 to 0.21875
Outputs:
- token_grad: bfloat16 [16384, 2048], P(('dp', 'expert'), 'mp')
- gate_grad: float32 [8, 704, 2048], P('expert', 'mp', 'dp')
- up_grad: float32 [8, 704, 2048], P('expert', 'mp', 'dp')
- down_grad: float32 [8, 704, 2048], P('expert', 'mp', 'dp')
The draws below stay inside these ranges and needn't reach their ends.
Inputs may be any that keep to these rules, and one draw needn't show every extreme that they name: `routes`: each row names 2 different experts. In every block of 128 consecutive rows (the tokens of one device) no expert is named by more than 48 rows, and some expert, drawn afresh for each block, is named by exactly 48 rows.
All inputs are finite; a program needn't handle non-finite values.
Results may differ from the reference program's by a relative error of at most 0.02.
Values may be sent and summed in bfloat16 or wider, within the bound.
A program may use at most 64 MiB of HBM per device.

```python
import jax
import jax.numpy as jnp
from jax import lax

D = 2048
HW = 704
TOP = 2
TOK_DEV = 128
EXPERTS = 8
CAP = 48
TOKENS = 16384
N_DP = 16
N_EXPERT = 8
N_MP = 4


def route_block(block_key):
    pair_total = TOK_DEV * TOP
    other_count = EXPERTS - 1
    remaining = pair_total - CAP
    base_load = remaining // other_count
    extra_load = remaining % other_count
    move_room = max(0, min(base_load, CAP - base_load - 1))
    key_order, key_moves, key_perm, key_turn, key_hot = jax.random.split(block_key, 5)
    hot_expert = jax.random.randint(key_hot, (), 0, EXPERTS)
    shuffle = jax.random.permutation(key_order, other_count)
    expert_load = base_load + (shuffle < extra_load).astype(jnp.int32)
    pair_count = other_count // 2
    if pair_count > 0:
        shifts = jax.random.randint(key_moves, (pair_count,), 0, move_room + 1)
        expert_load = expert_load.at[0:2 * pair_count:2].add(shifts)
        expert_load = expert_load.at[1:2 * pair_count:2].add(-shifts)
    other_ids = jnp.arange(other_count, dtype=jnp.int32)
    expert_ids = other_ids + (other_ids >= hot_expert).astype(jnp.int32)
    counts = jnp.zeros((EXPERTS,), jnp.int32).at[expert_ids].set(expert_load).at[hot_expert].set(CAP)
    run_ends = jnp.cumsum(counts)
    places = jnp.arange(pair_total, dtype=jnp.int32)
    sequence = jnp.sum((run_ends[None, :] <= places[:, None]).astype(jnp.int32), axis=1)
    route_table = sequence.reshape(TOP, TOK_DEV).T
    rotation = jax.random.randint(key_turn, (TOK_DEV, 1), 0, TOP)
    columns = (jnp.arange(TOP, dtype=jnp.int32)[None, :] + rotation) % TOP
    route_table = jnp.take_along_axis(route_table, columns, axis=1)
    permuted = jax.random.permutation(key_perm, TOK_DEV)
    return route_table[permuted].astype(jnp.int32)


def draw_routes(key, part):
    key = jax.random.fold_in(key, 7)
    block_keys = jax.random.split(jax.random.fold_in(key, 2), TOKENS // TOK_DEV)
    tables = jax.vmap(route_block)(block_keys)
    return tables.reshape(TOKENS, TOP)


def levels(key, extent, cuts, low, top_value):
    gain, own = 1.0, jax.random.fold_in(key, 6)
    for position, blocks in cuts:
        heights = jnp.exp(jax.random.uniform(jax.random.fold_in(own, position), (blocks,), jnp.float32, low / len(cuts), top_value / len(cuts)))
        gain = gain * jnp.repeat(heights, extent[position] // blocks).reshape([-1 if axis == position else 1 for axis in range(len(extent))])
    return gain


def normal_values(rng, extent, scale, bound, cuts=(), kind=jnp.bfloat16):
    values = scale * jax.random.normal(rng, extent, jnp.float32)
    if cuts:
        values = values * levels(rng, extent, cuts, -0.22, 0.18)
    return jnp.clip(values, -bound, bound).astype(kind)


def setup_inputs(seed: int = 0) -> dict:
    splits = jax.random.split(jax.random.key(seed), 8)
    return {
        "tokens": normal_values(splits[0], (TOKENS, D), 1.0, 6.0, ((0, 128),)),
        "out_grad": normal_values(splits[1], (TOKENS, D), 0.25, 1.5, ((0, 128),)),
        "routes": draw_routes(jax.random.fold_in(splits[7], 71), 0),
        "gate_values": jnp.clip(0.2 + 0.8 * jax.random.uniform(splits[3], (TOKENS, TOP), jnp.float32) ** levels(splits[3], (TOKENS, TOP), ((0, 128),), -0.2, 0.2), 0.2, 1.0),
        "gate_proj": normal_values(splits[4], (EXPERTS, HW, D), D ** -0.5, 0.125, ((0, 8), (1, 4), (2, 16))),
        "up_proj": normal_values(splits[5], (EXPERTS, HW, D), D ** -0.5, 0.125, ((0, 8), (1, 4), (2, 16))),
        "down_proj": normal_values(splits[6], (EXPERTS, HW, D), HW ** -0.5, 0.21875, ((0, 8), (1, 4), (2, 16))),
    }


def slot_table(route_rows):
    flat_ids = route_rows.reshape(-1)
    one_hot = (flat_ids[:, None] == jnp.arange(EXPERTS, dtype=jnp.int32)[None, :]).astype(jnp.int32)
    rank_in = jnp.sum(jnp.cumsum(one_hot, axis=0) * one_hot, axis=1) - 1
    return (flat_ids * CAP + rank_in).astype(jnp.int32)


def pack_rows(slot_ids, rows_in):
    return jnp.zeros((EXPERTS * CAP, D), rows_in.dtype).at[slot_ids].set(rows_in)


def expert_terms(rows_in, rows_grad, gate_full, up_full, down_full):
    pre_gate = jnp.dot(rows_in, gate_full.T, preferred_element_type=jnp.float32)
    pre_up = jnp.dot(rows_in, up_full.T, preferred_element_type=jnp.float32)
    sigmoid_gate = jax.nn.sigmoid(pre_gate)
    active = pre_gate * sigmoid_gate
    hidden = (active * pre_up).astype(jnp.bfloat16)
    back_hidden = jnp.dot(rows_grad, down_full.T, preferred_element_type=jnp.float32)
    back_gate = (back_hidden * pre_up * sigmoid_gate * (1.0 + pre_gate * (1.0 - sigmoid_gate))).astype(jnp.bfloat16)
    back_up = (back_hidden * active).astype(jnp.bfloat16)
    grad_gate = jnp.dot(back_gate.T, rows_in, preferred_element_type=jnp.float32)
    grad_up = jnp.dot(back_up.T, rows_in, preferred_element_type=jnp.float32)
    grad_down = jnp.dot(hidden.T, rows_grad, preferred_element_type=jnp.float32)
    slice_width = HW // N_MP
    row_sum = jnp.zeros(rows_in.shape, jnp.float32)
    for slice_index in range(N_MP):
        lower = slice_index * slice_width
        upper = lower + slice_width
        partial_rows = jnp.dot(back_gate[:, lower:upper], gate_full[lower:upper], preferred_element_type=jnp.float32)
        partial_rows = partial_rows + jnp.dot(back_up[:, lower:upper], up_full[lower:upper], preferred_element_type=jnp.float32)
        partial_rows = lax.optimization_barrier(partial_rows.astype(jnp.bfloat16))
        row_sum = row_sum + partial_rows.astype(jnp.float32)
    return grad_gate, grad_up, grad_down, row_sum.astype(jnp.bfloat16)


def reference(tokens, out_grad, routes, gate_values, gate_proj, up_proj, down_proj):
    groups = N_DP
    sources = N_EXPERT
    token_blocks = tokens.reshape(groups, sources, TOK_DEV, D)
    grad_blocks = out_grad.reshape(groups, sources, TOK_DEV, D)
    route_blocks = routes.reshape(groups, sources, TOK_DEV, TOP)
    value_blocks = gate_values.reshape(groups, sources, TOK_DEV * TOP, 1)

    def round_trip(grad_part):
        return lax.optimization_barrier(grad_part.astype(jnp.bfloat16)).astype(jnp.float32)

    def group_step(totals, pieces):
        token_rows, grad_rows, route_rows, value_rows = pieces
        slot_ids = jax.vmap(slot_table)(route_rows)
        copied = jnp.repeat(token_rows, TOP, axis=1)
        scaled = (value_rows * jnp.repeat(grad_rows, TOP, axis=1).astype(jnp.float32)).astype(jnp.bfloat16)
        send_in = jax.vmap(pack_rows)(slot_ids, copied)
        send_grad = jax.vmap(pack_rows)(slot_ids, scaled)
        recv_in = send_in.reshape(sources, EXPERTS, CAP, D).transpose(1, 0, 2, 3).reshape(EXPERTS, sources * CAP, D)
        recv_grad = send_grad.reshape(sources, EXPERTS, CAP, D).transpose(1, 0, 2, 3).reshape(EXPERTS, sources * CAP, D)

        def per_expert(expert_items):
            return expert_terms(expert_items[0], expert_items[1], expert_items[2], expert_items[3], expert_items[4])

        grad_gate, grad_up, grad_down, row_grads = lax.map(per_expert, (recv_in, recv_grad, gate_proj, up_proj, down_proj))
        new_totals = (totals[0] + round_trip(grad_gate), totals[1] + round_trip(grad_up), totals[2] + round_trip(grad_down))
        returned = row_grads.reshape(EXPERTS, sources, CAP, D).transpose(1, 0, 2, 3).reshape(sources, EXPERTS * CAP, D)
        picked = jax.vmap(lambda rows_back, slot_row: rows_back[slot_row])(returned, slot_ids)
        combined = jnp.sum(picked.astype(jnp.float32).reshape(sources, TOK_DEV, TOP, D), axis=2).astype(jnp.bfloat16)
        return new_totals, combined

    zero_grads = jnp.zeros((EXPERTS, HW, D), jnp.float32)
    totals, combined = lax.scan(group_step, (zero_grads, zero_grads, zero_grads), (token_blocks, grad_blocks, route_blocks, value_blocks))
    return combined.reshape(TOKENS, D), totals[0], totals[1], totals[2]
```

```python
import functools

import jax
import jax.numpy as jnp
from jax import lax
from jax.experimental import pallas as pl
from jax.experimental.pallas import tpu as pltpu
from jax.sharding import PartitionSpec as P

MESH = pl.DeviceIdType.MESH
F32 = jnp.float32
BF16 = jnp.bfloat16

SHIFTS = (0, 1, 7, 2, 6, 3, 5, 4)
SLOTS = 8
CAP = 48
HID = 176
HID3 = 3 * HID
CUT = 272
PIECES = ((0, CUT), (CUT, HID3 - CUT))


def dot(a, b, ca, cb):
    return lax.dot_general(a, b, (((ca,), (cb,)), ((), ())), preferred_element_type=F32)


def kernel(
    tok_hbm, grad_hbm, routes_ref, gates_ref, gate_hbm, up_hbm, down_hbm,
    tok_out, gate_out, up_out, down_out,
    tokq, gradq, pack, sendq, rows, weights, back, hid, row_grad, wgrad, sib_rs, ring_in, ring_out, xs_in, yback, ret,
    loc, y_s, y_r, x_s, x_r, ag_s, ag_r, sg_s, sg_r, xs_s, xs_r, yb_s, yb_r, sr_s, sr_r, rr_s, rr_r,
):
    d, e, m = lax.axis_index("dp"), lax.axis_index("expert"), lax.axis_index("mp")
    z, c = d // 2, d % 2
    width = tokq.shape[1]

    def at_z(shift, core=None):
        return ((((z + shift) % 8) * 2 + (c if core is None else core)), e, m)

    def at_y(shift):
        return (d, (e + shift) % 8, m)

    def at_x(shift):
        return (d, e, (m + shift) % 4)

    z_right, z_left, sibling = at_z(1), at_z(7), at_z(0, 1 - c)
    x_right, x_left, x_far = at_x(1), at_x(3), at_x(2)

    def quarter(shift):
        return pl.ds(pl.multiple_of(((m + shift) % 4) * width, width), width)

    def block(shift, core):
        return pl.ds(pl.multiple_of((((z + shift) % 8) * 2 + core) * 128, 128), 128)

    def remote(src, dst, send, recv, device):
        return pltpu.make_async_remote_copy(
            src_ref=src, dst_ref=dst, send_sem=send, recv_sem=recv, device_id=device, device_id_type=MESH
        )

    pending = []

    def send(src, dst, send_sem, recv_sem, device):
        copy = remote(src, dst, send_sem, recv_sem, device)
        copy.start()
        pending.append(copy)

    def arrived(dst, send_sem, recv_sem, device):
        remote(dst, dst, send_sem, recv_sem, device).wait_recv()

    barrier = pltpu.get_barrier_semaphore()
    partners = [z_right, z_left, sibling, x_right, x_left, x_far] + [at_y(k) for k in range(1, 8)]
    for partner in partners:
        pl.semaphore_signal(barrier, inc=1, device_id=partner, device_id_type=MESH)

    own = block(0, c)
    loads = [
        pltpu.make_async_copy(tok_hbm.at[:, quarter(0)], tokq, loc.at[0]),
        pltpu.make_async_copy(grad_hbm.at[:, quarter(0)], gradq, loc.at[1]),
        pltpu.make_async_copy(gate_hbm.at[0], weights.at[pl.ds(0, HID), own], loc.at[2]),
        pltpu.make_async_copy(up_hbm.at[0], weights.at[pl.ds(HID, HID), own], loc.at[3]),
        pltpu.make_async_copy(down_hbm.at[0], weights.at[pl.ds(2 * HID, HID), own], loc.at[4]),
    ]
    for copy in loads:
        copy.start()

    count = tokq.shape[0]
    slot_id = lax.broadcasted_iota(jnp.int32, (SLOTS, count), 0)
    wanted = jnp.zeros((SLOTS, count), jnp.int32)
    for j, shift in enumerate(SHIFTS):
        wanted = jnp.where(slot_id == j, (e + shift) % 8, wanted)
    first = routes_ref[0:1, :] == wanted
    second = routes_ref[1:2, :] == wanted
    named = jnp.where(first, 1.0, jnp.where(second, 1.0, 0.0))
    value = jnp.where(first, gates_ref[0:1, :], jnp.where(second, gates_ref[1:2, :], 0.0))
    earlier = jnp.where(
        lax.broadcasted_iota(jnp.int32, (count, count), 0) < lax.broadcasted_iota(jnp.int32, (count, count), 1),
        1.0, 0.0,
    ).astype(BF16)
    rank = dot(named.astype(BF16), earlier, 1, 0).astype(jnp.int32)
    place = jnp.where(named > 0.5, rank, -1)
    row_id = lax.broadcasted_iota(jnp.int32, (CAP, count), 0)
    scales = []
    for j in range(SLOTS):
        taken = place[j : j + 1, :] == row_id
        pack[pl.ds(j * CAP, CAP), :] = jnp.where(taken, 1.0, 0.0).astype(BF16)
        scales.append(jnp.sum(jnp.where(taken, value[j : j + 1, :], 0.0), axis=1, keepdims=True))

    loads[0].wait()
    loads[1].wait()

    def pack_slots(lo, hi):
        chosen = pack[pl.ds(lo * CAP, (hi - lo) * CAP), :]
        taken_rows = dot(chosen, tokq[...], 1, 0).astype(BF16)
        taken_grads = dot(chosen, gradq[...], 1, 0)
        for j in range(lo, hi):
            part = slice((j - lo) * CAP, (j - lo + 1) * CAP)
            sendq[j, 0:CAP, :] = taken_rows[part]
            sendq[j, CAP : 2 * CAP, :] = (taken_grads[part] * scales[j]).astype(BF16)

    def y_send(j):
        send(sendq.at[j], rows.at[j, :, quarter(0)], y_s.at[j], y_r.at[j], at_y(SHIFTS[j]))

    def x_send(j):
        src = sendq.at[0] if j == 0 else rows.at[j, :, quarter(0)]
        send(src, rows.at[j, :, quarter(0)], x_s.at[j, 0], x_r.at[j, 0], x_right)
        send(src, rows.at[j, :, quarter(0)], x_s.at[j, 1], x_r.at[j, 1], x_left)

    def x_forward(j):
        arrived(rows.at[j, :, quarter(3)], x_s.at[j, 0], x_r.at[j, 0], x_left)
        part = rows.at[j, pl.ds(0, CAP), quarter(3)]
        send(part, part, x_s.at[j, 2], x_r.at[j, 2], x_right)
        arrived(rows.at[j, :, quarter(1)], x_s.at[j, 1], x_r.at[j, 1], x_right)
        part = rows.at[j, pl.ds(CAP, CAP), quarter(1)]
        send(part, part, x_s.at[j, 3], x_r.at[j, 3], x_left)

    def x_complete(j):
        arrived(rows.at[j, pl.ds(0, CAP), quarter(2)], x_s.at[j, 2], x_r.at[j, 2], x_left)
        arrived(rows.at[j, pl.ds(CAP, CAP), quarter(2)], x_s.at[j, 3], x_r.at[j, 3], x_right)

    def weight_part(shift, core, half):
        if half is None:
            return weights.at[:, block(shift, core)]
        return weights.at[pl.ds(*PIECES[half]), block(shift, core)]

    def ag_send(step, side):
        shift = (8 - (step - 1)) % 8 if side == 0 else step - 1
        part = weight_part(shift, c, side if step == 4 else None)
        send(part, part, ag_s.at[side, step - 1], ag_r.at[side, step - 1], z_right if side == 0 else z_left)

    def sib_send(index, shift, half=None):
        part = weight_part(shift, c, half)
        send(part, part, sg_s.at[index], sg_r.at[index], sibling)

    def ag_step(step):
        for side in (0, 1):
            shift = 8 - step if side == 0 else step
            half = side if step == 4 else None
            arrived(
                weight_part(shift, c, half), ag_s.at[side, step - 1], ag_r.at[side, step - 1],
                z_left if side == 0 else z_right,
            )
            if step < 4:
                ag_send(step + 1, side)
            sib_send(1 + 2 * (step - 1) + side, shift, half)

    def weights_complete():
        arrived(weight_part(0, 1 - c, None), sg_s.at[0], sg_r.at[0], sibling)
        for step in range(1, 5):
            for side in (0, 1):
                shift = 8 - step if side == 0 else step
                half = side if step == 4 else None
                index = 1 + 2 * (step - 1) + side
                arrived(weight_part(shift, 1 - c, half), sg_s.at[index], sg_r.at[index], sibling)

    def batch(b, lo, lanes=slice(None)):
        part = rows[4 * b : 4 * b + 4, lo : lo + CAP, lanes]
        return part.reshape(4 * CAP, part.shape[2])

    def forward(b):
        pre = dot(weights[0 : 2 * HID, :], batch(b, 0), 1, 1)
        back_hidden = dot(weights[2 * HID : HID3, :], batch(b, CAP), 1, 1)
        pre_gate, pre_up = pre[0:HID], pre[HID : 2 * HID]
        s = jax.nn.sigmoid(pre_gate)
        active = pre_gate * s
        hid[b] = (active * pre_up).astype(BF16)
        back[b, 0:HID] = (back_hidden * pre_up * s * (1.0 + pre_gate * (1.0 - s))).astype(BF16)
        back[b, HID : 2 * HID] = (back_hidden * active).astype(BF16)

    def row_grads(b):
        for q in range(4):
            lanes = slice(q * width, (q + 1) * width)
            part = dot(back[b], weights[0 : 2 * HID, lanes], 0, 0).astype(BF16)
            row_grad[4 * b : 4 * b + 4, :, lanes] = part.reshape(4, CAP, width)

    def rs_send(j):
        for index, (shift, device) in enumerate(((1, x_right), (3, x_left), (2, x_far))):
            send(
                row_grad.at[j, :, quarter(shift)], xs_in.at[j, index], xs_s.at[j, index], xs_r.at[j, index], device,
            )

    def rs_finish(j):
        total = row_grad[j, :, quarter(0)].astype(F32)
        for index, device in enumerate((x_left, x_right, x_far)):
            arrived(xs_in.at[j, index], xs_s.at[j, index], xs_r.at[j, index], device)
            total = total + xs_in[j, index].astype(F32)
        if j == 0:
            ret[0] = total.astype(BF16)
        else:
            yback[j] = total.astype(BF16)
            send(yback.at[j], ret.at[j], yb_s.at[j], yb_r.at[j], at_y(8 - SHIFTS[j]))

    def weight_chunk(index, shift):
        lanes = pl.ds(pl.multiple_of(((z + shift) % 8) * 256, 256), 256)
        grad_gu = dot(back[0], batch(0, 0, lanes), 1, 0) + dot(back[1], batch(1, 0, lanes), 1, 0)
        grad_d = dot(hid[0], batch(0, CAP, lanes), 1, 0) + dot(hid[1], batch(1, CAP, lanes), 1, 0)
        wgrad[0 : 2 * HID, lanes] = grad_gu.astype(BF16)
        wgrad[2 * HID : HID3, lanes] = grad_d.astype(BF16)
        send(wgrad.at[:, block(shift, 1 - c)], sib_rs.at[index], sr_s.at[index], sr_r.at[index], sibling)

    chunk_shifts = (4, 3, 5, 2, 6, 1, 7, 0)

    def pair_ready(index):
        arrived(sib_rs.at[index], sr_s.at[index], sr_r.at[index], sibling)

    def pair_sum(index, lo, size):
        mine = wgrad[pl.ds(lo, size), block(chunk_shifts[index], c)].astype(F32)
        return mine + sib_rs[index, pl.ds(lo, size), :].astype(F32)

    def ring_part(ref, side, step, piece):
        return ref.at[side, step - 1, pl.ds(*PIECES[piece])]

    def ring_send(step, side, piece, total):
        lo, size = PIECES[piece]
        ring_out[side, step - 1, pl.ds(lo, size), :] = total.astype(BF16)
        send(
            ring_part(ring_out, side, step, piece), ring_part(ring_in, side, step, piece),
            rr_s.at[side, step - 1, piece], rr_r.at[side, step - 1, piece], z_right if side == 0 else z_left,
        )

    def ring_recv(step, side, piece):
        lo, size = PIECES[piece]
        arrived(
            ring_part(ring_in, side, step, piece), rr_s.at[side, step - 1, piece], rr_r.at[side, step - 1, piece],
            z_left if side == 0 else z_right,
        )
        return ring_in[side, step - 1, pl.ds(lo, size), :].astype(F32)

    def ring_step(step):
        if step == 1:
            pair_ready(0)
            for side in (0, 1):
                ring_send(1, side, side, pair_sum(0, *PIECES[side]))
            return
        for side in (0, 1):
            pair_ready(2 * step - 3 + side)
        for turn in (0, 1):
            for side in (0, 1):
                piece = side if turn == 0 else 1 - side
                total = pair_sum(2 * step - 3 + side, *PIECES[piece])
                if step > 2 or piece == side:
                    total = total + ring_recv(step - 1, side, piece)
                ring_send(step, side, piece, total)

    pack_slots(0, 4)
    for copy in loads[2:]:
        copy.wait()
    pl.semaphore_wait(barrier, len(partners))

    for j in (1, 2, 3, 4):
        if j == 4:
            pack_slots(4, 8)
        y_send(j)
    x_send(0)
    keep = pltpu.make_async_copy(sendq.at[0], rows.at[0, :, quarter(0)], loc.at[5])
    keep.start()
    ag_send(1, 0)
    ag_send(1, 1)
    sib_send(0, 0)

    for i in range(1, 9):
        if i < 8:
            arrived(rows.at[i, :, quarter(0)], y_s.at[i], y_r.at[i], at_y(8 - SHIFTS[i]))
            x_send(i)
            if i + 4 < 8:
                y_send(i + 4)
        x_forward(i - 1)
        if i <= 4:
            ag_step(i)
        if i >= 2:
            x_complete(i - 2)
        if i == 6:
            keep.wait()
            weights_complete()
            forward(0)
        if i == 7:
            row_grads(0)
    for j in (0, 1, 2, 3):
        rs_send(j)
    x_complete(7)

    forward(1)
    for index, shift in enumerate(chunk_shifts):
        weight_chunk(index, shift)
        if index == 2:
            ring_step(1)
    row_grads(1)
    for j in (7, 6, 5, 4):
        rs_send(j)
    rs_finish(0)
    rs_finish(1)
    ring_step(2)
    rs_finish(2)
    rs_finish(3)
    ring_step(3)
    rs_finish(7)
    rs_finish(6)
    ring_step(4)
    rs_finish(5)
    rs_finish(4)
    for j in range(1, SLOTS):
        arrived(ret.at[j], yb_s.at[j], yb_r.at[j], at_y(SHIFTS[j]))
    back_rows = ret[...].reshape(SLOTS * CAP, width)
    tok_out[...] = dot(pack[...], back_rows, 0, 0).astype(BF16)

    pair_ready(7)
    totals = []
    for piece in (0, 1):
        totals.append(pair_sum(7, *PIECES[piece]) + ring_recv(4, 0, piece) + ring_recv(4, 1, piece))
    gate_out[0] = totals[0][0:HID]
    up_out[0, 0 : CUT - HID] = totals[0][HID:CUT]
    up_out[0, CUT - HID : HID] = totals[1][0 : 2 * HID - CUT]
    down_out[0] = totals[1][2 * HID - CUT :]

    for copy in pending:
        copy.wait_send()


def on_device(tokens, out_grad, routes, gate_values, gate_proj, up_proj, down_proj):
    count, model = tokens.shape
    width = model // lax.axis_size("mp")
    sems = pltpu.SemaphoreType.DMA
    vmem = pl.BlockSpec(memory_space=pltpu.VMEM)
    hbm = pl.BlockSpec(memory_space=pl.ANY)
    weight_out = jax.ShapeDtypeStruct(gate_proj.shape, F32)
    return pl.pallas_call(
        kernel,
        out_shape=(jax.ShapeDtypeStruct((count, width), BF16), weight_out, weight_out, weight_out),
        in_specs=[hbm, hbm, vmem, vmem, hbm, hbm, hbm],
        out_specs=(vmem, vmem, vmem, vmem),
        scratch_shapes=[
            pltpu.VMEM((count, width), BF16),
            pltpu.VMEM((count, width), BF16),
            pltpu.VMEM((SLOTS * CAP, count), BF16),
            pltpu.VMEM((SLOTS, 2 * CAP, width), BF16),
            pltpu.VMEM((SLOTS, 2 * CAP, model), BF16),
            pltpu.VMEM((HID3, model), BF16),
            pltpu.VMEM((2, 2 * HID, 4 * CAP), BF16),
            pltpu.VMEM((2, HID, 4 * CAP), BF16),
            pltpu.VMEM((SLOTS, CAP, model), BF16),
            pltpu.VMEM((HID3, model), BF16),
            pltpu.VMEM((8, HID3, 128), BF16),
            pltpu.VMEM((2, 4, HID3, 128), BF16),
            pltpu.VMEM((2, 4, HID3, 128), BF16),
            pltpu.VMEM((SLOTS, 3, CAP, width), BF16),
            pltpu.VMEM((SLOTS, CAP, width), BF16),
            pltpu.VMEM((SLOTS, CAP, width), BF16),
            sems((6,)),
            sems((SLOTS,)),
            sems((SLOTS,)),
            sems((SLOTS, 4)),
            sems((SLOTS, 4)),
            sems((2, 4)),
            sems((2, 4)),
            sems((9,)),
            sems((9,)),
            sems((SLOTS, 3)),
            sems((SLOTS, 3)),
            sems((SLOTS,)),
            sems((SLOTS,)),
            sems((8,)),
            sems((8,)),
            sems((2, 4, 2)),
            sems((2, 4, 2)),
        ],
        compiler_params=pltpu.CompilerParams(
            collective_id=0, has_side_effects=True, vmem_limit_bytes=40 * 1024 * 1024
        ),
        cost_estimate=pl.CostEstimate(flops=2300000000, bytes_accessed=4000000, transcendentals=70000),
        name="experts",
    )(tokens, out_grad, routes.T, gate_values.T, gate_proj, up_proj, down_proj)


def solution(mesh):
    tokens_in = P(("dp", "expert"), None)
    weights_in = P("expert", "mp", "dp")
    return jax.shard_map(
        on_device,
        mesh=mesh,
        in_specs=(tokens_in, tokens_in, tokens_in, tokens_in, weights_in, weights_in, weights_in),
        out_specs=(P(("dp", "expert"), "mp"), weights_in, weights_in, weights_in),
        check_vma=False,
    )
```

```python
import functools

import jax
import jax.numpy as jnp
from jax import lax
from jax.experimental import pallas as pl
from jax.experimental.pallas import tpu as pltpu
from jax.sharding import PartitionSpec as P

MESH = pl.DeviceIdType.MESH
F32 = jnp.float32
BF16 = jnp.bfloat16

SHIFTS = (0, 2, 6, 3, 5, 4, 1, 7)
SLOTS = 8
FAR = 6
NEAR = (6, 7)
BATCHES = ((0, 3), (3, 8))
CAP = 48
HID = 176
HID3 = 3 * HID
HALVES = ((0, 272), (272, 256))
PIECES = ((0, 144), (144, 128), (272, 128), (400, 128))


def dot(a, b, ca, cb):
    return lax.dot_general(a, b, (((ca,), (cb,)), ((), ())), preferred_element_type=F32)


def kernel(
    tok_hbm, grad_hbm, routes_hbm, gates_hbm, gate_hbm, up_hbm, down_hbm,
    tok_out, gate_out, up_out, down_out,
    tokq, gradq, tokf, gradf, routes_ref, gates_ref, pack, sendq, sendf, rows, weights, back_a, back_b, hid_a, hid_b,
    row_grad, wacc, wgrad, sib_rs, ring_in, ring_out, xs_in, yback, ret,
    loc, y_s, y_r, x_s, x_r, ag_s, ag_r, sg_s, sg_r, xs_s, xs_r, yb_s, yb_r, sr_s, sr_r, rr_s, rr_r,
):
    d, e, m = lax.axis_index("dp"), lax.axis_index("expert"), lax.axis_index("mp")
    z, c = d // 2, d % 2
    width = tokq.shape[1]

    def at_z(shift, core=None):
        return ((((z + shift) % 8) * 2 + (c if core is None else core)), e, m)

    def at_y(shift):
        return (d, (e + shift) % 8, m)

    def at_x(shift):
        return (d, e, (m + shift) % 4)

    z_right, z_left, sibling = at_z(1), at_z(7), at_z(0, 1 - c)
    x_right, x_left, x_far = at_x(1), at_x(3), at_x(2)

    def quarter(shift):
        return pl.ds(pl.multiple_of(((m + shift) % 4) * width, width), width)

    def block(shift, core):
        return pl.ds(pl.multiple_of((((z + shift) % 8) * 2 + core) * 128, 128), 128)

    def remote(src, dst, send, recv, device):
        return pltpu.make_async_remote_copy(
            src_ref=src, dst_ref=dst, send_sem=send, recv_sem=recv, device_id=device, device_id_type=MESH
        )

    pending = []

    def send(src, dst, send_sem, recv_sem, device):
        copy = remote(src, dst, send_sem, recv_sem, device)
        copy.start()
        pending.append(copy)

    def arrived(dst, send_sem, recv_sem, device):
        remote(dst, dst, send_sem, recv_sem, device).wait_recv()

    barrier = pltpu.get_barrier_semaphore()
    partners = [z_right, z_left, sibling, x_right, x_left, x_far] + [at_y(k) for k in range(1, 8)]
    for partner in partners:
        pl.semaphore_signal(barrier, inc=1, device_id=partner, device_id_type=MESH)

    own = block(0, c)
    loads = [
        pltpu.make_async_copy(routes_hbm, routes_ref, loc.at[0]),
        pltpu.make_async_copy(gates_hbm, gates_ref, loc.at[1]),
        pltpu.make_async_copy(tok_hbm.at[:, quarter(0)], tokq, loc.at[2]),
        pltpu.make_async_copy(grad_hbm.at[:, quarter(0)], gradq, loc.at[3]),
        pltpu.make_async_copy(gate_hbm.at[0], weights.at[pl.ds(0, HID), own], loc.at[4]),
        pltpu.make_async_copy(up_hbm.at[0], weights.at[pl.ds(HID, HID), own], loc.at[5]),
        pltpu.make_async_copy(down_hbm.at[0], weights.at[pl.ds(2 * HID, HID), own], loc.at[6]),
        pltpu.make_async_copy(tok_hbm, tokf, loc.at[7]),
        pltpu.make_async_copy(grad_hbm, gradf, loc.at[8]),
    ]
    for copy in loads:
        copy.start()

    loads[0].wait()
    loads[1].wait()
    count = tokq.shape[0]
    slot_id = lax.broadcasted_iota(jnp.int32, (SLOTS, count), 0)
    wanted = jnp.zeros((SLOTS, count), jnp.int32)
    for j, shift in enumerate(SHIFTS):
        wanted = jnp.where(slot_id == j, (e + shift) % 8, wanted)
    first = routes_ref[0:1, :] == wanted
    second = routes_ref[1:2, :] == wanted
    named = jnp.where(first, 1.0, jnp.where(second, 1.0, 0.0))
    value = jnp.where(first, gates_ref[0:1, :], jnp.where(second, gates_ref[1:2, :], 0.0))
    earlier = jnp.where(
        lax.broadcasted_iota(jnp.int32, (count, count), 0) < lax.broadcasted_iota(jnp.int32, (count, count), 1),
        1.0, 0.0,
    ).astype(BF16)
    rank = dot(named.astype(BF16), earlier, 1, 0).astype(jnp.int32)
    place = jnp.where(named > 0.5, rank, -1)
    row_id = lax.broadcasted_iota(jnp.int32, (CAP, count), 0)
    scales = []
    for j in range(SLOTS):
        taken = place[j : j + 1, :] == row_id
        pack[pl.ds(j * CAP, CAP), :] = jnp.where(taken, 1.0, 0.0).astype(BF16)
        scales.append(jnp.sum(jnp.where(taken, value[j : j + 1, :], 0.0), axis=1, keepdims=True))

    def packed(lo, hi, tok, grad):
        chosen = pack[pl.ds(lo * CAP, (hi - lo) * CAP), :]
        taken_rows = dot(chosen, tok[...], 1, 0).astype(BF16)
        taken_grads = dot(chosen, grad[...], 1, 0)
        for j in range(lo, hi):
            part = slice((j - lo) * CAP, (j - lo + 1) * CAP)
            yield j, taken_rows[part], (taken_grads[part] * scales[j]).astype(BF16)

    def y_send(j):
        if j in NEAR:
            send(sendf.at[j - FAR], rows.at[j], y_s.at[j], y_r.at[j], at_y(SHIFTS[j]))
        else:
            send(sendq.at[j - 1], rows.at[j, :, quarter(0)], y_s.at[j], y_r.at[j], at_y(SHIFTS[j]))

    def y_arrived(j):
        part = rows.at[j] if j in NEAR else rows.at[j, :, quarter(0)]
        arrived(part, y_s.at[j], y_r.at[j], at_y(8 - SHIFTS[j]))

    def x_send(j):
        part = rows.at[j, :, quarter(0)]
        send(part, part, x_s.at[j - 1, 0], x_r.at[j - 1, 0], x_right)
        send(part, part, x_s.at[j - 1, 1], x_r.at[j - 1, 1], x_left)

    def x_forward(j):
        arrived(rows.at[j, :, quarter(3)], x_s.at[j - 1, 0], x_r.at[j - 1, 0], x_left)
        part = rows.at[j, pl.ds(0, CAP), quarter(3)]
        send(part, part, x_s.at[j - 1, 2], x_r.at[j - 1, 2], x_right)
        arrived(rows.at[j, :, quarter(1)], x_s.at[j - 1, 1], x_r.at[j - 1, 1], x_right)
        part = rows.at[j, pl.ds(CAP, CAP), quarter(1)]
        send(part, part, x_s.at[j - 1, 3], x_r.at[j - 1, 3], x_left)

    def x_complete(j):
        arrived(rows.at[j, pl.ds(0, CAP), quarter(2)], x_s.at[j - 1, 2], x_r.at[j - 1, 2], x_left)
        arrived(rows.at[j, pl.ds(CAP, CAP), quarter(2)], x_s.at[j - 1, 3], x_r.at[j - 1, 3], x_right)

    def weight_part(shift, core, half):
        if half is None:
            return weights.at[:, block(shift, core)]
        return weights.at[pl.ds(*HALVES[half]), block(shift, core)]

    def ag_shift(step, side):
        return (8 - step) % 8 if side == 0 else step

    def ag_halves(step, side):
        return (side,) if step == 4 else (0, 1)

    def ag_send(step, side, half):
        part = weight_part(ag_shift(step - 1, side), c, half)
        device = z_right if side == 0 else z_left
        send(part, part, ag_s.at[side, step - 1, half], ag_r.at[side, step - 1, half], device)

    def sib_half(step, side):
        return side if step == 4 else None

    def sib_send(step, side):
        index = 1 + 2 * (step - 1) + side if step else 0
        part = weight_part(ag_shift(step, side), c, sib_half(step, side))
        send(part, part, sg_s.at[index], sg_r.at[index], sibling)

    def ag_start():
        for half in (0, 1):
            for side in (0, 1):
                ag_send(1, side, half)
        sib_send(0, 0)

    def ag_step(step):
        for half in (0, 1):
            for side in (0, 1):
                if half in ag_halves(step, side):
                    arrived(
                        weight_part(ag_shift(step, side), c, half), ag_s.at[side, step - 1, half],
                        ag_r.at[side, step - 1, half], z_left if side == 0 else z_right,
                    )
                    if step < 4 and half in ag_halves(step + 1, side):
                        ag_send(step + 1, side, half)
        for side in (0, 1):
            sib_send(step, side)

    def weights_complete():
        arrived(weight_part(0, 1 - c, None), sg_s.at[0], sg_r.at[0], sibling)
        for step in range(1, 5):
            for side in (0, 1):
                index = 1 + 2 * (step - 1) + side
                part = weight_part(ag_shift(step, side), 1 - c, sib_half(step, side))
                arrived(part, sg_s.at[index], sg_r.at[index], sibling)

    backs, hids = (back_a, back_b), (hid_a, hid_b)

    def batch(b, lo, lanes=slice(None)):
        first, last = BATCHES[b]
        part = rows[first:last, lo : lo + CAP, lanes]
        return part.reshape((last - first) * CAP, part.shape[2])

    def forward(b):
        pre = dot(weights[0 : 2 * HID, :], batch(b, 0), 1, 1)
        back_hidden = dot(weights[2 * HID : HID3, :], batch(b, CAP), 1, 1)
        pre_gate, pre_up = pre[0:HID], pre[HID : 2 * HID]
        s = jax.nn.sigmoid(pre_gate)
        active = pre_gate * s
        hids[b][...] = (active * pre_up).astype(BF16)
        backs[b][0:HID, :] = (back_hidden * pre_up * s * (1.0 + pre_gate * (1.0 - s))).astype(BF16)
        backs[b][HID : 2 * HID, :] = (back_hidden * active).astype(BF16)

    def row_grads(b):
        first, last = BATCHES[b]
        for q in range(4):
            lanes = slice(q * width, (q + 1) * width)
            part = dot(backs[b][...], weights[0 : 2 * HID, lanes], 0, 0).astype(BF16)
            row_grad[first:last, :, lanes] = part.reshape(last - first, CAP, width)

    def rs_send(j):
        for index, (shift, device) in enumerate(((1, x_right), (3, x_left), (2, x_far))):
            send(
                row_grad.at[j, :, quarter(shift)], xs_in.at[j, index], xs_s.at[j, index], xs_r.at[j, index], device,
            )

    def rs_finish(j):
        total = row_grad[j, :, quarter(0)].astype(F32)
        for index, device in enumerate((x_left, x_right, x_far)):
            arrived(xs_in.at[j, index], xs_s.at[j, index], xs_r.at[j, index], device)
            total = total + xs_in[j, index].astype(F32)
        if j == 0:
            ret[0] = total.astype(BF16)
        else:
            yback[j] = total.astype(BF16)
            send(yback.at[j], ret.at[j], yb_s.at[j], yb_r.at[j], at_y(8 - SHIFTS[j]))

    def weight_early():
        for k in range(8):
            lanes = slice(256 * k, 256 * (k + 1))
            wacc[0 : 2 * HID, lanes] = dot(back_a[...], batch(0, 0, lanes), 1, 0)
            wacc[2 * HID : HID3, lanes] = dot(hid_a[...], batch(0, CAP, lanes), 1, 0)

    def weight_chunk(index, shift):
        lanes = pl.ds(pl.multiple_of(((z + shift) % 8) * 256, 256), 256)
        grad_gu = wacc[0 : 2 * HID, lanes] + dot(back_b[...], batch(1, 0, lanes), 1, 0)
        grad_d = wacc[2 * HID : HID3, lanes] + dot(hid_b[...], batch(1, CAP, lanes), 1, 0)
        wgrad[0 : 2 * HID, lanes] = grad_gu.astype(BF16)
        wgrad[2 * HID : HID3, lanes] = grad_d.astype(BF16)
        send(wgrad.at[:, block(shift, 1 - c)], sib_rs.at[index], sr_s.at[index], sr_r.at[index], sibling)

    chunk_shifts = (4, 3, 5, 2, 6, 1, 7, 0)

    def pair_ready(index):
        arrived(sib_rs.at[index], sr_s.at[index], sr_r.at[index], sibling)

    def pair_sum(index, lo, size):
        mine = wgrad[pl.ds(lo, size), block(chunk_shifts[index], c)].astype(F32)
        return mine + sib_rs[index, pl.ds(lo, size), :].astype(F32)

    def ring_part(ref, side, step, piece):
        return ref.at[side, step - 1, pl.ds(*PIECES[piece])]

    def ring_send(step, side, piece, total):
        lo, size = PIECES[piece]
        ring_out[side, step - 1, pl.ds(lo, size), :] = total.astype(BF16)
        send(
            ring_part(ring_out, side, step, piece), ring_part(ring_in, side, step, piece),
            rr_s.at[side, step - 1, piece], rr_r.at[side, step - 1, piece], z_right if side == 0 else z_left,
        )

    def ring_recv(step, side, piece):
        lo, size = PIECES[piece]
        arrived(
            ring_part(ring_in, side, step, piece), rr_s.at[side, step - 1, piece], rr_r.at[side, step - 1, piece],
            z_left if side == 0 else z_right,
        )
        return ring_in[side, step - 1, pl.ds(lo, size), :].astype(F32)

    def ring_step(step):
        if step == 1:
            pair_ready(0)
            for turn in (0, 1):
                for side in (0, 1):
                    piece = 2 * side + turn
                    ring_send(1, side, piece, pair_sum(0, *PIECES[piece]))
            return
        for side in (0, 1):
            pair_ready(2 * step - 3 + side)
        for turn in range(4):
            for side in (0, 1):
                piece = (turn + 2 * side) % 4
                total = pair_sum(2 * step - 3 + side, *PIECES[piece])
                if step > 2 or piece // 2 == side:
                    total = total + ring_recv(step - 1, side, piece)
                ring_send(step, side, piece, total)

    loads[2].wait()
    loads[3].wait()
    for j, part, grad_part in packed(1, FAR, tokq, gradq):
        sendq[j - 1, 0:CAP, :] = part
        sendq[j - 1, CAP : 2 * CAP, :] = grad_part
    pl.semaphore_wait(barrier, len(partners))

    for j in (1, 2, 3, 4):
        y_send(j)
    for copy in loads[4:7]:
        copy.wait()
    ag_start()
    loads[7].wait()
    loads[8].wait()
    for j, part, grad_part in packed(0, 1, tokf, gradf):
        rows[0, 0:CAP, :] = part
        rows[0, CAP : 2 * CAP, :] = grad_part
    for j, part, grad_part in packed(FAR, SLOTS, tokf, gradf):
        sendf[j - FAR, 0:CAP, :] = part
        sendf[j - FAR, CAP : 2 * CAP, :] = grad_part

    ag_step(1)
    for j in (1, 2):
        y_arrived(j)
        x_send(j)
    y_send(5)
    ag_step(2)
    x_forward(1)
    x_forward(2)
    for j in (3, 4):
        y_arrived(j)
        x_send(j)
    for j in NEAR:
        y_send(j)
    ag_step(3)
    y_arrived(5)
    x_send(5)
    x_complete(1)
    x_complete(2)
    ag_step(4)
    x_forward(3)
    x_forward(4)
    weights_complete()
    forward(0)
    x_forward(5)
    row_grads(0)
    for j in range(*BATCHES[0]):
        rs_send(j)
    weight_early()
    for j in (3, 4, 5):
        x_complete(j)
    for j in NEAR:
        y_arrived(j)

    forward(1)
    row_grads(1)
    for j in (5, 3, 4, 6, 7):
        rs_send(j)
    for index, shift in enumerate(chunk_shifts):
        weight_chunk(index, shift)
        if index == 1:
            ring_step(1)
    for j in (1, 2, 0):
        rs_finish(j)
    ring_step(2)
    rs_finish(5)
    rs_finish(3)
    ring_step(3)
    rs_finish(4)
    rs_finish(6)
    ring_step(4)
    rs_finish(7)

    pair_ready(7)
    outs = ((0, HID, gate_out), (HID, 2 * HID, up_out), (2 * HID, HID3, down_out))
    for piece in range(4):
        lo, size = PIECES[piece]
        total = pair_sum(7, lo, size) + ring_recv(4, 0, piece) + ring_recv(4, 1, piece)
        for first, last, out in outs:
            start, stop = max(first, lo), min(last, lo + size)
            if start < stop:
                out[0, start - first : stop - first] = total[start - lo : stop - lo]

    for j in range(1, SLOTS):
        arrived(ret.at[j], yb_s.at[j], yb_r.at[j], at_y(SHIFTS[j]))
    back_rows = ret[...].reshape(SLOTS * CAP, width)
    tok_out[...] = dot(pack[...], back_rows, 0, 0).astype(BF16)

    for copy in pending:
        copy.wait_send()


def on_device(tokens, out_grad, routes, gate_values, gate_proj, up_proj, down_proj):
    count, model = tokens.shape
    width = model // lax.axis_size("mp")
    sems = pltpu.SemaphoreType.DMA
    vmem = pl.BlockSpec(memory_space=pltpu.VMEM)
    hbm = pl.BlockSpec(memory_space=pltpu.HBM)
    weight_out = jax.ShapeDtypeStruct(gate_proj.shape, F32)
    return pl.pallas_call(
        kernel,
        out_shape=(jax.ShapeDtypeStruct((count, width), BF16), weight_out, weight_out, weight_out),
        in_specs=[hbm] * 7,
        out_specs=(vmem, vmem, vmem, vmem),
        scratch_shapes=[
            pltpu.VMEM((count, width), BF16),
            pltpu.VMEM((count, width), BF16),
            pltpu.VMEM((count, model), BF16),
            pltpu.VMEM((count, model), BF16),
            pltpu.VMEM((2, count), jnp.int32),
            pltpu.VMEM((2, count), F32),
            pltpu.VMEM((SLOTS * CAP, count), BF16),
            pltpu.VMEM((FAR - 1, 2 * CAP, width), BF16),
            pltpu.VMEM((len(NEAR), 2 * CAP, model), BF16),
            pltpu.VMEM((SLOTS, 2 * CAP, model), BF16),
            pltpu.VMEM((HID3, model), BF16),
            *(pltpu.VMEM((2 * HID, (last - first) * CAP), BF16) for first, last in BATCHES),
            *(pltpu.VMEM((HID, (last - first) * CAP), BF16) for first, last in BATCHES),
            pltpu.VMEM((SLOTS, CAP, model), BF16),
            pltpu.VMEM((HID3, model), F32),
            pltpu.VMEM((HID3, model), BF16),
            pltpu.VMEM((8, HID3, 128), BF16),
            pltpu.VMEM((2, 4, HID3, 128), BF16),
            pltpu.VMEM((2, 4, HID3, 128), BF16),
            pltpu.VMEM((SLOTS, 3, CAP, width), BF16),
            pltpu.VMEM((SLOTS, CAP, width), BF16),
            pltpu.VMEM((SLOTS, CAP, width), BF16),
            sems((9,)),
            sems((SLOTS,)),
            sems((SLOTS,)),
            sems((FAR - 1, 4)),
            sems((FAR - 1, 4)),
            sems((2, 4, 2)),
            sems((2, 4, 2)),
            sems((9,)),
            sems((9,)),
            sems((SLOTS, 3)),
            sems((SLOTS, 3)),
            sems((SLOTS,)),
            sems((SLOTS,)),
            sems((8,)),
            sems((8,)),
            sems((2, 4, 4)),
            sems((2, 4, 4)),
        ],
        compiler_params=pltpu.CompilerParams(
            collective_id=0, has_side_effects=True, vmem_limit_bytes=56 * 1024 * 1024
        ),
        cost_estimate=pl.CostEstimate(flops=2300000000, bytes_accessed=4000000, transcendentals=70000),
        name="experts",
    )(tokens, out_grad, routes.T, gate_values.T, gate_proj, up_proj, down_proj)


def solution(mesh):
    tokens_in = P(("dp", "expert"), None)
    weights_in = P("expert", "mp", "dp")
    return jax.shard_map(
        on_device,
        mesh=mesh,
        in_specs=(tokens_in, tokens_in, tokens_in, tokens_in, weights_in, weights_in, weights_in),
        out_specs=(P(("dp", "expert"), "mp"), weights_in, weights_in, weights_in),
        check_vma=False,
    )
```

```python
import functools

import jax
import jax.numpy as jnp
from jax import lax
from jax.experimental import pallas as pl
from jax.experimental.pallas import tpu as pltpu
from jax.sharding import PartitionSpec as P

MESH = pl.DeviceIdType.MESH
F32 = jnp.float32
BF16 = jnp.bfloat16

SHIFTS = (0, 2, 6, 3, 5, 4, 1, 7)
SLOTS = 8
FAR = 6
NEAR = (6, 7)
SPLIT = (1, 2, 3, 4)
LAST_FAR = 5
BATCHES = ((0, 3), (3, 5), (5, 6), (6, 8))
GROUPS = ((1, 3),)
CAP = 48
HID = 176
HID3 = 3 * HID
HALVES = ((0, 272), (272, 256))
PIECES = ((0, 144), (144, 128), (272, 128), (400, 128))


def dot(a, b, ca, cb):
    return lax.dot_general(a, b, (((ca,), (cb,)), ((), ())), preferred_element_type=F32)


def kernel(
    tok_hbm, grad_hbm, routes_hbm, gates_hbm, gate_hbm, up_hbm, down_hbm,
    tok_out, gate_out, up_out, down_out,
    tokq, gradq, tokf, gradf, routes_ref, gates_ref, pack, sendq, sendf, rows, weights, back_a, back_b, hid_a, hid_b,
    row_grad, wacc, wgrad, sib_rs, ring_in, ring_out, xs_in, gr_in, gx_in, yback, ret,
    loc, y_s, y_r, x_s, x_r, ag_s, ag_r, sg_s, sg_r, xs_s, xs_r, gs_s, gs_r, yb_s, yb_r, sr_s, sr_r, rr_s, rr_r,
):
    d, e, m = lax.axis_index("dp"), lax.axis_index("expert"), lax.axis_index("mp")
    z, c = d // 2, d % 2
    width = tokq.shape[1]

    def at_z(shift, core=None):
        return ((((z + shift) % 8) * 2 + (c if core is None else core)), e, m)

    def at_y(shift):
        return (d, (e + shift) % 8, m)

    def at_x(shift):
        return (d, e, (m + shift) % 4)

    z_right, z_left, sibling = at_z(1), at_z(7), at_z(0, 1 - c)
    z_right2, z_left2 = at_z(2), at_z(6)
    x_right, x_left, x_far = at_x(1), at_x(3), at_x(2)

    def quarter(shift):
        return pl.ds(pl.multiple_of(((m + shift) % 4) * width, width), width)

    def block(shift, core):
        return pl.ds(pl.multiple_of((((z + shift) % 8) * 2 + core) * 128, 128), 128)

    def remote(src, dst, send, recv, device):
        return pltpu.make_async_remote_copy(
            src_ref=src, dst_ref=dst, send_sem=send, recv_sem=recv, device_id=device, device_id_type=MESH
        )

    pending = []

    def send(src, dst, send_sem, recv_sem, device):
        copy = remote(src, dst, send_sem, recv_sem, device)
        copy.start()
        pending.append(copy)

    def arrived(dst, send_sem, recv_sem, device):
        remote(dst, dst, send_sem, recv_sem, device).wait_recv()

    barrier = pltpu.get_barrier_semaphore()
    partners = [z_right, z_left, z_right2, z_left2, sibling, x_right, x_left, x_far] + [at_y(k) for k in range(1, 8)]
    for partner in partners:
        pl.semaphore_signal(barrier, inc=1, device_id=partner, device_id_type=MESH)

    own = block(0, c)
    loads = [
        pltpu.make_async_copy(routes_hbm, routes_ref, loc.at[0]),
        pltpu.make_async_copy(gates_hbm, gates_ref, loc.at[1]),
        pltpu.make_async_copy(tok_hbm.at[:, quarter(0)], tokq, loc.at[2]),
        pltpu.make_async_copy(grad_hbm.at[:, quarter(0)], gradq, loc.at[3]),
        pltpu.make_async_copy(gate_hbm.at[0], weights.at[pl.ds(0, HID), own], loc.at[4]),
        pltpu.make_async_copy(up_hbm.at[0], weights.at[pl.ds(HID, HID), own], loc.at[5]),
        pltpu.make_async_copy(down_hbm.at[0], weights.at[pl.ds(2 * HID, HID), own], loc.at[6]),
        pltpu.make_async_copy(tok_hbm, tokf, loc.at[7]),
        pltpu.make_async_copy(grad_hbm, gradf, loc.at[8]),
    ]
    for copy in loads:
        copy.start()

    loads[0].wait()
    loads[1].wait()
    count = tokq.shape[0]
    slot_id = lax.broadcasted_iota(jnp.int32, (SLOTS, count), 0)
    wanted = jnp.zeros((SLOTS, count), jnp.int32)
    for j, shift in enumerate(SHIFTS):
        wanted = jnp.where(slot_id == j, (e + shift) % 8, wanted)
    first = routes_ref[0:1, :] == wanted
    second = routes_ref[1:2, :] == wanted
    named = jnp.where(first, 1.0, jnp.where(second, 1.0, 0.0))
    value = jnp.where(first, gates_ref[0:1, :], jnp.where(second, gates_ref[1:2, :], 0.0))
    earlier = jnp.where(
        lax.broadcasted_iota(jnp.int32, (count, count), 0) < lax.broadcasted_iota(jnp.int32, (count, count), 1),
        1.0, 0.0,
    ).astype(BF16)
    rank = dot(named.astype(BF16), earlier, 1, 0).astype(jnp.int32)
    place = jnp.where(named > 0.5, rank, -1)
    row_id = lax.broadcasted_iota(jnp.int32, (CAP, count), 0)
    scales = []
    for j in range(SLOTS):
        taken = place[j : j + 1, :] == row_id
        pack[pl.ds(j * CAP, CAP), :] = jnp.where(taken, 1.0, 0.0).astype(BF16)
        scales.append(jnp.sum(jnp.where(taken, value[j : j + 1, :], 0.0), axis=1, keepdims=True))

    def packed(lo, hi, tok, grad):
        chosen = pack[pl.ds(lo * CAP, (hi - lo) * CAP), :]
        taken_rows = dot(chosen, tok[...], 1, 0).astype(BF16)
        taken_grads = dot(chosen, grad[...], 1, 0)
        for j in range(lo, hi):
            part = slice((j - lo) * CAP, (j - lo + 1) * CAP)
            yield j, taken_rows[part], (taken_grads[part] * scales[j]).astype(BF16)

    both, token_rows, grad_rows = pl.ds(0, 2 * CAP), pl.ds(0, CAP), pl.ds(CAP, CAP)

    def y_send(j, part=0, span=both):
        if j in NEAR:
            send(sendf.at[j - FAR], rows.at[j], y_s.at[j, 0], y_r.at[j, 0], at_y(SHIFTS[j]))
        else:
            send(
                sendq.at[j - 1, span], rows.at[j, span, quarter(0)], y_s.at[j, part], y_r.at[j, part], at_y(SHIFTS[j]),
            )

    def y_arrived(j, part=0, span=both):
        where = rows.at[j] if j in NEAR else rows.at[j, span, quarter(0)]
        arrived(where, y_s.at[j, part], y_r.at[j, part], at_y(8 - SHIFTS[j]))

    def x_send(j, part=0, span=both):
        block_out = rows.at[j, span, quarter(0)]
        send(block_out, block_out, x_s.at[j - 1, part, 0], x_r.at[j - 1, part, 0], x_right)
        send(block_out, block_out, x_s.at[j - 1, part, 1], x_r.at[j - 1, part, 1], x_left)
        if j == LAST_FAR:
            send(block_out, block_out, x_s.at[j - 1, part, 2], x_r.at[j - 1, part, 2], x_far)

    def x_arrived(j, side, part=0, span=both):
        shift, device = ((3, x_left), (1, x_right), (2, x_far))[side]
        arrived(rows.at[j, span, quarter(shift)], x_s.at[j - 1, part, side], x_r.at[j - 1, part, side], device)

    def forward_send(j, side):
        block_out = rows.at[j, grad_rows if side else token_rows, quarter(1 if side else 3)]
        device = x_left if side else x_right
        send(block_out, block_out, x_s.at[j - 1, side, 2], x_r.at[j - 1, side, 2], device)

    def x_forward(j, side):
        if j in SPLIT:
            x_arrived(j, side, side, (token_rows, grad_rows)[side])
        else:
            x_arrived(j, side)
        forward_send(j, side)

    def x_complete(j):
        if j == LAST_FAR:
            for side in (0, 1, 2):
                x_arrived(j, side)
            return
        if j in SPLIT:
            x_arrived(j, 1, 0, token_rows)
            x_arrived(j, 0, 1, grad_rows)
        arrived(rows.at[j, token_rows, quarter(2)], x_s.at[j - 1, 0, 2], x_r.at[j - 1, 0, 2], x_left)
        arrived(rows.at[j, grad_rows, quarter(2)], x_s.at[j - 1, 1, 2], x_r.at[j - 1, 1, 2], x_right)

    def weight_part(shift, core, half):
        if half is None:
            return weights.at[:, block(shift, core)]
        return weights.at[pl.ds(*HALVES[half]), block(shift, core)]

    def ag_shift(step, side):
        return (8 - step) % 8 if side == 0 else step

    def ag_halves(step, side):
        return (side,) if step == 4 else (0, 1)

    def ag_send(step, side, half):
        part = weight_part(ag_shift(step - 1, side), c, half)
        device = z_right if side == 0 else z_left
        send(part, part, ag_s.at[side, step - 1, half], ag_r.at[side, step - 1, half], device)

    def sib_half(step, side):
        return side if step == 4 else None

    def sib_send(step, side):
        index = 1 + 2 * (step - 1) + side if step else 0
        part = weight_part(ag_shift(step, side), c, sib_half(step, side))
        send(part, part, sg_s.at[index], sg_r.at[index], sibling)

    def ag_start():
        for copy in loads[4:7]:
            copy.wait()
        for half in (0, 1):
            for side in (0, 1):
                ag_send(1, side, half)
        sib_send(0, 0)

    def ag_step(step):
        for half in (0, 1):
            for side in (0, 1):
                if half in ag_halves(step, side):
                    arrived(
                        weight_part(ag_shift(step, side), c, half), ag_s.at[side, step - 1, half],
                        ag_r.at[side, step - 1, half], z_left if side == 0 else z_right,
                    )
                    if step < 4 and half in ag_halves(step + 1, side):
                        ag_send(step + 1, side, half)
        for side in (0, 1):
            sib_send(step, side)

    def weights_complete():
        arrived(weight_part(0, 1 - c, None), sg_s.at[0], sg_r.at[0], sibling)
        for step in range(1, 5):
            for side in (0, 1):
                index = 1 + 2 * (step - 1) + side
                part = weight_part(ag_shift(step, side), 1 - c, sib_half(step, side))
                arrived(part, sg_s.at[index], sg_r.at[index], sibling)

    def hidden_terms(b):
        first, last = BATCHES[b]
        base = 0 if b == 0 else BATCHES[1][0]
        lanes = slice((first - base) * CAP, (last - base) * CAP)
        return (back_a, hid_a, lanes) if b == 0 else (back_b, hid_b, lanes)


    def batch(first, last, lo, lanes=slice(None)):
        part = rows[first:last, lo : lo + CAP, lanes]
        return part.reshape((last - first) * CAP, part.shape[2])

    def forward(b):
        first, last = BATCHES[b]
        pre = dot(weights[0 : 2 * HID, :], batch(first, last, 0), 1, 1)
        back_hidden = dot(weights[2 * HID : HID3, :], batch(first, last, CAP), 1, 1)
        pre_gate, pre_up = pre[0:HID], pre[HID : 2 * HID]
        s = jax.nn.sigmoid(pre_gate)
        active = pre_gate * s
        back_ref, hid_ref, lanes = hidden_terms(b)
        hid_ref[:, lanes] = (active * pre_up).astype(BF16)
        back_ref[0:HID, lanes] = (back_hidden * pre_up * s * (1.0 + pre_gate * (1.0 - s))).astype(BF16)
        back_ref[HID : 2 * HID, lanes] = (back_hidden * active).astype(BF16)

    def row_grads(b):
        first, last = BATCHES[b]
        back_ref, _, terms = hidden_terms(b)
        for q in range(4):
            lanes = slice(q * width, (q + 1) * width)
            part = dot(back_ref[:, terms], weights[0 : 2 * HID, lanes], 0, 0).astype(BF16)
            row_grad[first:last, :, lanes] = part.reshape(last - first, CAP, width)

    def rs_send(j):
        for index, (shift, device) in enumerate(((1, x_right), (3, x_left), (2, x_far))):
            send(
                row_grad.at[j, :, quarter(shift)], xs_in.at[j, index], xs_s.at[j, index], xs_r.at[j, index], device,
            )

    def rs_finish(j):
        total = row_grad[j, :, quarter(0)].astype(F32)
        for index, device in enumerate((x_left, x_right, x_far)):
            arrived(xs_in.at[j, index], xs_s.at[j, index], xs_r.at[j, index], device)
            total = total + xs_in[j, index].astype(F32)
        if j == 0:
            ret[0] = total.astype(BF16)
        else:
            yback[j] = total.astype(BF16)
            send(yback.at[j], ret.at[j], yb_s.at[j], yb_r.at[j], at_y(8 - SHIFTS[j]))

    def half_quarter(shift, side):
        return pl.ds(pl.multiple_of(((m + shift) % 4) * width + side * (width // 2), width // 2), width // 2)

    def group_start(g):
        first, last = GROUPS[g]
        for side, device in enumerate((x_right, x_left)):
            send(
                row_grad.at[first:last, :, half_quarter(2, side)], gr_in.at[side, first:last],
                gs_s.at[g, side], gs_r.at[g, side], device,
            )

    def group_pass(g):
        first, last = GROUPS[g]
        for side, (shift, device, source) in enumerate(((1, x_right, x_left), (3, x_left, x_right))):
            arrived(gr_in.at[side, first:last], gs_s.at[g, side], gs_r.at[g, side], source)
            lanes = half_quarter(shift, side)
            for j in range(first, last):
                total = row_grad[j, :, lanes].astype(F32) + gr_in[side, j].astype(F32)
                row_grad[j, :, lanes] = total.astype(BF16)
            send(
                row_grad.at[first:last, :, quarter(shift)], gx_in.at[side, first:last],
                gs_s.at[g, 2 + side], gs_r.at[g, 2 + side], device,
            )

    def group_finish(g):
        first, last = GROUPS[g]
        for side, source in enumerate((x_left, x_right)):
            arrived(gx_in.at[side, first:last], gs_s.at[g, 2 + side], gs_r.at[g, 2 + side], source)
        for j in range(first, last):
            total = row_grad[j, :, quarter(0)].astype(F32) + gx_in[0, j].astype(F32) + gx_in[1, j].astype(F32)
            yback[j] = total.astype(BF16)
            send(yback.at[j], ret.at[j], yb_s.at[j], yb_r.at[j], at_y(8 - SHIFTS[j]))

    def weight_early():
        first, last = BATCHES[0]
        for k in range(8):
            lanes = slice(256 * k, 256 * (k + 1))
            wacc[0 : 2 * HID, lanes] = dot(back_a[...], batch(first, last, 0, lanes), 1, 0)
            wacc[2 * HID : HID3, lanes] = dot(hid_a[...], batch(first, last, CAP, lanes), 1, 0)

    def weight_chunk(index):
        shift = chunk_shifts[index]
        first, last = BATCHES[1][0], SLOTS
        lanes = pl.ds(pl.multiple_of(((z + shift) % 8) * 256, 256), 256)
        grad_gu = wacc[0 : 2 * HID, lanes] + dot(back_b[...], batch(first, last, 0, lanes), 1, 0)
        grad_d = wacc[2 * HID : HID3, lanes] + dot(hid_b[...], batch(first, last, CAP, lanes), 1, 0)
        wgrad[0 : 2 * HID, lanes] = grad_gu.astype(BF16)
        wgrad[2 * HID : HID3, lanes] = grad_d.astype(BF16)
        send(wgrad.at[:, block(shift, 1 - c)], sib_rs.at[index], sr_s.at[index], sr_r.at[index], sibling)

    chunk_shifts = (4, 3, 5, 2, 6, 1, 7, 0)

    def pair_ready(index):
        arrived(sib_rs.at[index], sr_s.at[index], sr_r.at[index], sibling)

    def pair_sum(index, lo, size):
        mine = wgrad[pl.ds(lo, size), block(chunk_shifts[index], c)].astype(F32)
        return mine + sib_rs[index, pl.ds(lo, size), :].astype(F32)

    def ring_part(ref, side, slot, piece):
        return ref.at[side, slot, pl.ds(*PIECES[piece])]

    def ring_send(side, slot, piece, total):
        lo, size = PIECES[piece]
        ring_out[side, slot, pl.ds(lo, size), :] = total.astype(BF16)
        send(
            ring_part(ring_out, side, slot, piece), ring_part(ring_in, side, slot, piece),
            rr_s.at[side, slot, piece], rr_r.at[side, slot, piece],
            ((z_right, z_left), (z_right2, z_left2))[slot == 0][side],
        )

    def ring_recv(side, slot, piece):
        lo, size = PIECES[piece]
        arrived(
            ring_part(ring_in, side, slot, piece), rr_s.at[side, slot, piece], rr_r.at[side, slot, piece],
            ((z_left, z_right), (z_left2, z_right2))[slot == 0][side],
        )
        return ring_in[side, slot, pl.ds(lo, size), :].astype(F32)

    def ring_order():
        for turn in range(4):
            for side in (0, 1):
                yield side, (turn + 2 * (1 - side)) % 4

    def ring_far():
        pair_ready(0)
        for turn in (0, 1):
            for side in (0, 1):
                piece = 2 * side + turn
                ring_send(side, 0, piece, pair_sum(0, *PIECES[piece]))

    def ring_first():
        for side in (0, 1):
            pair_ready(1 + side)
        for side, piece in ring_order():
            ring_send(side, 1, piece, pair_sum(1 + side, *PIECES[piece]))

    def ring_step(slot, half):
        if half == 0:
            for side in (0, 1):
                pair_ready(2 * slot - 1 + side)
        for side, piece in tuple(ring_order())[4 * half : 4 * half + 4]:
            total = pair_sum(2 * slot - 1 + side, *PIECES[piece]) + ring_recv(side, slot - 1, piece)
            if slot == 2 and piece // 2 == side:
                total = total + ring_recv(side, 0, piece)
            ring_send(side, slot, piece, total)

    def weight_outputs():
        pair_ready(7)
        outs = ((0, HID, gate_out), (HID, 2 * HID, up_out), (2 * HID, HID3, down_out))
        for piece in range(4):
            lo, size = PIECES[piece]
            total = pair_sum(7, lo, size) + ring_recv(0, 3, piece) + ring_recv(1, 3, piece)
            for first, last, out in outs:
                start, stop = max(first, lo), min(last, lo + size)
                if start < stop:
                    out[0, start - first : stop - first] = total[start - lo : stop - lo]

    def token_outputs():
        for j in range(1, SLOTS):
            arrived(ret.at[j], yb_s.at[j], yb_r.at[j], at_y(SHIFTS[j]))
        back_rows = ret[...].reshape(SLOTS * CAP, width)
        tok_out[...] = dot(pack[...], back_rows, 0, 0).astype(BF16)

    def pack_full():
        loads[7].wait()
        loads[8].wait()
        for j, part, grad_part in packed(0, 1, tokf, gradf):
            rows[0, 0:CAP, :] = part
            rows[0, CAP : 2 * CAP, :] = grad_part
        for j, part, grad_part in packed(FAR, SLOTS, tokf, gradf):
            sendf[j - FAR, 0:CAP, :] = part
            sendf[j - FAR, CAP : 2 * CAP, :] = grad_part

    def pack_quarter(lo, hi):
        for j, part, grad_part in packed(lo, hi, tokq, gradq):
            sendq[j - 1, 0:CAP, :] = part
            sendq[j - 1, CAP : 2 * CAP, :] = grad_part

    loads[2].wait()
    loads[3].wait()
    pack_quarter(1, 3)
    pl.semaphore_wait(barrier, len(partners))

    y_send(1, 1, grad_rows)
    y_send(2, 0, token_rows)
    y_send(1, 0, token_rows)
    ag_start()
    pack_quarter(3, FAR)
    pack_full()
    y_send(2, 1, grad_rows)
    y_send(4, 1, grad_rows)
    y_send(4, 0, token_rows)
    y_send(3, 0, token_rows)
    y_arrived(2, 0, token_rows)
    x_send(2, 0, token_rows)
    ag_step(1)
    y_send(3, 1, grad_rows)
    y_send(5)
    y_arrived(1, 1, grad_rows)
    x_send(1, 1, grad_rows)
    y_arrived(1, 0, token_rows)
    x_send(1, 0, token_rows)
    y_send(7)
    y_arrived(2, 1, grad_rows)
    x_send(2, 1, grad_rows)
    y_arrived(3, 0, token_rows)
    x_send(3, 0, token_rows)
    y_arrived(4, 1, grad_rows)
    x_send(4, 1, grad_rows)
    ag_step(2)
    x_forward(2, 1)
    x_forward(1, 0)
    y_send(6)
    y_arrived(3, 1, grad_rows)
    x_send(3, 1, grad_rows)
    y_arrived(4, 0, token_rows)
    x_send(4, 0, token_rows)
    x_forward(4, 1)
    x_forward(2, 0)
    ag_step(3)
    x_forward(3, 0)
    x_forward(1, 1)
    x_forward(3, 1)
    x_forward(4, 0)
    y_arrived(5)
    x_send(5)
    x_complete(1)
    x_complete(2)
    ag_step(4)
    weights_complete()
    x_complete(3)
    forward(0)
    x_complete(4)
    row_grads(0)
    group_start(0)
    forward(1)
    row_grads(1)
    rs_send(3)
    weight_early()
    y_arrived(7)
    y_arrived(6)
    forward(3)
    rs_send(4)
    x_complete(5)
    forward(2)
    weight_chunk(0)
    row_grads(2)
    group_pass(0)
    weight_chunk(1)
    weight_chunk(2)
    ring_far()
    rs_send(5)
    ring_first()
    row_grads(3)
    rs_finish(3)
    weight_chunk(3)
    rs_send(7)
    rs_send(6)
    rs_finish(4)
    rs_send(0)
    weight_chunk(4)
    weight_chunk(5)
    group_finish(0)
    weight_chunk(6)
    weight_chunk(7)
    ring_step(2, 0)
    ring_step(2, 1)
    rs_finish(5)
    ring_step(3, 0)
    rs_finish(7)
    ring_step(3, 1)
    rs_finish(6)
    rs_finish(0)
    weight_outputs()
    token_outputs()

    for copy in pending:
        copy.wait_send()


def finish(tok_ref, gate_ref, up_ref, down_ref, tok_out, gate_out, up_out, down_out):
    tok_out[...] = tok_ref[...]
    gate_out[...] = gate_ref[...]
    up_out[...] = up_ref[...]
    down_out[...] = down_ref[...]


def on_device(tokens, out_grad, routes, gate_values, gate_proj, up_proj, down_proj):
    count, model = tokens.shape
    width = model // lax.axis_size("mp")
    sems = pltpu.SemaphoreType.DMA
    early = BATCHES[0][1]
    vmem = pl.BlockSpec(memory_space=pltpu.VMEM)
    hbm = pl.BlockSpec(memory_space=pltpu.HBM)
    weight_out = jax.ShapeDtypeStruct(gate_proj.shape, F32)
    results = pl.pallas_call(
        kernel,
        out_shape=(jax.ShapeDtypeStruct((count, width), BF16), weight_out, weight_out, weight_out),
        in_specs=[hbm] * 7,
        out_specs=(vmem, vmem, vmem, vmem),
        scratch_shapes=[
            pltpu.VMEM((count, width), BF16),
            pltpu.VMEM((count, width), BF16),
            pltpu.VMEM((count, model), BF16),
            pltpu.VMEM((count, model), BF16),
            pltpu.VMEM((2, count), jnp.int32),
            pltpu.VMEM((2, count), F32),
            pltpu.VMEM((SLOTS * CAP, count), BF16),
            pltpu.VMEM((FAR - 1, 2 * CAP, width), BF16),
            pltpu.VMEM((len(NEAR), 2 * CAP, model), BF16),
            pltpu.VMEM((SLOTS, 2 * CAP, model), BF16),
            pltpu.VMEM((HID3, model), BF16),
            pltpu.VMEM((2 * HID, early * CAP), BF16),
            pltpu.VMEM((2 * HID, (SLOTS - early) * CAP), BF16),
            pltpu.VMEM((HID, early * CAP), BF16),
            pltpu.VMEM((HID, (SLOTS - early) * CAP), BF16),
            pltpu.VMEM((SLOTS, CAP, model), BF16),
            pltpu.VMEM((HID3, model), F32),
            pltpu.VMEM((HID3, model), BF16),
            pltpu.VMEM((8, HID3, 128), BF16),
            pltpu.VMEM((2, 4, HID3, 128), BF16),
            pltpu.VMEM((2, 4, HID3, 128), BF16),
            pltpu.VMEM((SLOTS, 3, CAP, width), BF16),
            pltpu.VMEM((2, SLOTS, CAP, width // 2), BF16),
            pltpu.VMEM((2, SLOTS, CAP, width), BF16),
            pltpu.VMEM((SLOTS, CAP, width), BF16),
            pltpu.VMEM((SLOTS, CAP, width), BF16),
            sems((9,)),
            sems((FAR + len(NEAR), 2)),
            sems((FAR + len(NEAR), 2)),
            sems((FAR - 1, 2, 3)),
            sems((FAR - 1, 2, 3)),
            sems((2, 4, 2)),
            sems((2, 4, 2)),
            sems((9,)),
            sems((9,)),
            sems((SLOTS, 3)),
            sems((SLOTS, 3)),
            sems((len(GROUPS), 4)),
            sems((len(GROUPS), 4)),
            sems((SLOTS,)),
            sems((SLOTS,)),
            sems((8,)),
            sems((8,)),
            sems((2, 4, 4)),
            sems((2, 4, 4)),
        ],
        compiler_params=pltpu.CompilerParams(
            collective_id=0, has_side_effects=True, vmem_limit_bytes=56 * 1024 * 1024
        ),
        cost_estimate=pl.CostEstimate(flops=2300000000, bytes_accessed=4000000, transcendentals=70000),
        name="experts",
    )(tokens, out_grad, routes.T, gate_values.T, gate_proj, up_proj, down_proj)
    return pl.pallas_call(
        finish,
        out_shape=tuple(jax.ShapeDtypeStruct(result.shape, result.dtype) for result in results),
        in_specs=[vmem] * 4,
        out_specs=(vmem,) * 4,
        name="finish",
    )(*results)


def solution(mesh):
    tokens_in = P(("dp", "expert"), None)
    weights_in = P("expert", "mp", "dp")
    return jax.shard_map(
        on_device,
        mesh=mesh,
        in_specs=(tokens_in, tokens_in, tokens_in, tokens_in, weights_in, weights_in, weights_in),
        out_specs=(P(("dp", "expert"), "mp"), weights_in, weights_in, weights_in),
        check_vma=False,
    )
```

```python
import functools

import jax
import jax.numpy as jnp
from jax import lax
from jax.experimental import pallas as pl
from jax.experimental.pallas import tpu as pltpu
from jax.sharding import PartitionSpec as P

MESH = pl.DeviceIdType.MESH
F32 = jnp.float32
BF16 = jnp.bfloat16

SHIFTS = (0, 2, 6, 3, 5, 4, 1, 7)
SLOTS = 8
FAR = 6
NEAR = (6, 7)
SPLIT = (1, 2, 3, 4)
LAST_FAR = 5
BATCHES = ((0, 3), (3, 5), (5, 8))
GROUPS = ((1, 3), (3, 5))
CAP = 48
HID = 176
HID3 = 3 * HID
HALVES = ((0, 272), (272, 256))
PIECES = ((0, 144), (144, 128), (272, 128), (400, 128))


SENDS = 36
RECVS = 124


class Numbered:
    def __init__(self, sems, table, kind):
        self.sems, self.table, self.kind = sems, table, kind

    @property
    def at(self):
        return self

    def __getitem__(self, key):
        return self.sems.at[self.table.setdefault((self.kind, key), len(self.table))]


def dot(a, b, ca, cb):
    return lax.dot_general(a, b, (((ca,), (cb,)), ((), ())), preferred_element_type=F32)


def kernel(
    tok_hbm, grad_hbm, routes_hbm, gates_hbm, gate_hbm, up_hbm, down_hbm,
    tok_out, gate_out, up_out, down_out,
    tokq, gradq, tokf, gradf, routes_ref, gates_ref, pack, sendq, sendf, rows, weights, back_a, back_b, hid_a, hid_b,
    row_grad, wacc, wgrad, sib_rs, ring_in, ring_out, xs_in, gr_in, gx_in, yback, ret,
    loc, send_sems, recv_sems,
):
    table = {}
    kinds = [Numbered(recv_sems, table, kind) for kind in range(9)]
    y_r, x_r, ag_r, sg_r, xs_r, gs_r, yb_r, sr_r, rr_r = kinds
    d, e, m = lax.axis_index("dp"), lax.axis_index("expert"), lax.axis_index("mp")
    z, c = d // 2, d % 2
    width = tokq.shape[1]

    def at_z(shift, core=None):
        return ((((z + shift) % 8) * 2 + (c if core is None else core)), e, m)

    def at_y(shift):
        return (d, (e + shift) % 8, m)

    def at_x(shift):
        return (d, e, (m + shift) % 4)

    z_right, z_left, sibling = at_z(1), at_z(7), at_z(0, 1 - c)
    x_right, x_left, x_far = at_x(1), at_x(3), at_x(2)

    def quarter(shift):
        return pl.ds(pl.multiple_of(((m + shift) % 4) * width, width), width)

    def block(shift, core):
        return pl.ds(pl.multiple_of((((z + shift) % 8) * 2 + core) * 128, 128), 128)

    def remote(src, dst, send, recv, device):
        return pltpu.make_async_remote_copy(
            src_ref=src, dst_ref=dst, send_sem=send, recv_sem=recv, device_id=device, device_id_type=MESH
        )

    pending, free = [], list(range(SENDS))

    def drain(newest):
        while len(pending) > newest:
            copy, index = pending.pop(0)
            copy.wait_send()
            free.append(index)

    def send(src, dst, recv_sem, device):
        if not free:
            drain(SENDS - 1)
        index = free.pop(0)
        copy = remote(src, dst, send_sems.at[index], recv_sem, device)
        copy.start()
        pending.append((copy, index))

    def arrived(dst, recv_sem, device):
        remote(dst, dst, send_sems.at[0], recv_sem, device).wait_recv()

    barrier = pltpu.get_barrier_semaphore()
    partners = [z_right, z_left, sibling, x_right, x_left, x_far] + [at_y(k) for k in range(1, 8)]
    for partner in partners:
        pl.semaphore_signal(barrier, inc=1, device_id=partner, device_id_type=MESH)

    own = block(0, c)
    loads = [
        pltpu.make_async_copy(routes_hbm, routes_ref, loc.at[0]),
        pltpu.make_async_copy(gates_hbm, gates_ref, loc.at[1]),
        pltpu.make_async_copy(tok_hbm.at[:, quarter(0)], tokq, loc.at[2]),
        pltpu.make_async_copy(grad_hbm.at[:, quarter(0)], gradq, loc.at[3]),
        pltpu.make_async_copy(gate_hbm.at[0], weights.at[pl.ds(0, HID), own], loc.at[4]),
        pltpu.make_async_copy(up_hbm.at[0], weights.at[pl.ds(HID, HID), own], loc.at[5]),
        pltpu.make_async_copy(down_hbm.at[0], weights.at[pl.ds(2 * HID, HID), own], loc.at[6]),
        pltpu.make_async_copy(tok_hbm, tokf, loc.at[7]),
        pltpu.make_async_copy(grad_hbm, gradf, loc.at[8]),
    ]
    for copy in loads:
        copy.start()

    loads[0].wait()
    loads[1].wait()
    count = tokq.shape[0]
    slot_id = lax.broadcasted_iota(jnp.int32, (SLOTS, count), 0)
    wanted = jnp.zeros((SLOTS, count), jnp.int32)
    for j, shift in enumerate(SHIFTS):
        wanted = jnp.where(slot_id == j, (e + shift) % 8, wanted)
    first = routes_ref[0:1, :] == wanted
    second = routes_ref[1:2, :] == wanted
    named = jnp.where(first, 1.0, jnp.where(second, 1.0, 0.0))
    value = jnp.where(first, gates_ref[0:1, :], jnp.where(second, gates_ref[1:2, :], 0.0))
    earlier = jnp.where(
        lax.broadcasted_iota(jnp.int32, (count, count), 0) < lax.broadcasted_iota(jnp.int32, (count, count), 1),
        1.0, 0.0,
    ).astype(BF16)
    rank = dot(named.astype(BF16), earlier, 1, 0).astype(jnp.int32)
    place = jnp.where(named > 0.5, rank, -1)
    row_id = lax.broadcasted_iota(jnp.int32, (CAP, count), 0)
    scales = []
    for j in range(SLOTS):
        taken = place[j : j + 1, :] == row_id
        pack[pl.ds(j * CAP, CAP), :] = jnp.where(taken, 1.0, 0.0).astype(BF16)
        scales.append(jnp.sum(jnp.where(taken, value[j : j + 1, :], 0.0), axis=1, keepdims=True))

    def packed(lo, hi, tok, grad):
        chosen = pack[pl.ds(lo * CAP, (hi - lo) * CAP), :]
        taken_rows = dot(chosen, tok[...], 1, 0).astype(BF16)
        taken_grads = dot(chosen, grad[...], 1, 0)
        for j in range(lo, hi):
            part = slice((j - lo) * CAP, (j - lo + 1) * CAP)
            yield j, taken_rows[part], (taken_grads[part] * scales[j]).astype(BF16)

    both, token_rows, grad_rows = pl.ds(0, 2 * CAP), pl.ds(0, CAP), pl.ds(CAP, CAP)

    def y_send(j, part=0, span=both):
        if j in NEAR:
            send(sendf.at[j - FAR], rows.at[j], y_r.at[j, 0], at_y(SHIFTS[j]))
        else:
            send(
                sendq.at[j - 1, span], rows.at[j, span, quarter(0)], y_r.at[j, part], at_y(SHIFTS[j]),
            )

    def y_arrived(j, part=0, span=both):
        where = rows.at[j] if j in NEAR else rows.at[j, span, quarter(0)]
        arrived(where, y_r.at[j, part], at_y(8 - SHIFTS[j]))

    def x_send(j, part=0, span=both):
        block_out = rows.at[j, span, quarter(0)]
        send(block_out, block_out, x_r.at[j - 1, part, 0], x_right)
        send(block_out, block_out, x_r.at[j - 1, part, 1], x_left)
        if j == LAST_FAR:
            send(block_out, block_out, x_r.at[j - 1, part, 2], x_far)

    def x_arrived(j, side, part=0, span=both):
        shift, device = ((3, x_left), (1, x_right), (2, x_far))[side]
        arrived(rows.at[j, span, quarter(shift)], x_r.at[j - 1, part, side], device)

    def forward_send(j, side):
        block_out = rows.at[j, grad_rows if side else token_rows, quarter(1 if side else 3)]
        device = x_left if side else x_right
        send(block_out, block_out, x_r.at[j - 1, side, 2], device)

    def x_forward(j, side):
        if j in SPLIT:
            x_arrived(j, side, side, (token_rows, grad_rows)[side])
        else:
            x_arrived(j, side)
        forward_send(j, side)

    def x_complete(j):
        if j == LAST_FAR:
            for side in (0, 1, 2):
                x_arrived(j, side)
            return
        if j in SPLIT:
            x_arrived(j, 1, 0, token_rows)
            x_arrived(j, 0, 1, grad_rows)
        arrived(rows.at[j, token_rows, quarter(2)], x_r.at[j - 1, 0, 2], x_left)
        arrived(rows.at[j, grad_rows, quarter(2)], x_r.at[j - 1, 1, 2], x_right)

    def weight_part(shift, core, half):
        if half is None:
            return weights.at[:, block(shift, core)]
        return weights.at[pl.ds(*HALVES[half]), block(shift, core)]

    def ag_shift(step, side):
        return (8 - step) % 8 if side == 0 else step

    def ag_halves(step, side):
        return (side,) if step == 4 else (0, 1)

    def ag_send(step, side, half):
        part = weight_part(ag_shift(step - 1, side), c, half)
        device = z_right if side == 0 else z_left
        send(part, part, ag_r.at[side, step - 1, half], device)

    def sib_half(step, side):
        return side if step == 4 else None

    def sib_send(step, side):
        index = 1 + 2 * (step - 1) + side if step else 0
        part = weight_part(ag_shift(step, side), c, sib_half(step, side))
        send(part, part, sg_r.at[index], sibling)

    def ag_start():
        for copy in loads[4:7]:
            copy.wait()
        for half in (0, 1):
            for side in (0, 1):
                ag_send(1, side, half)
        sib_send(0, 0)

    def ag_step(step):
        for half in (0, 1):
            for side in (0, 1):
                if half in ag_halves(step, side):
                    arrived(
                        weight_part(ag_shift(step, side), c, half), ag_r.at[side, step - 1, half], z_left if side == 0 else z_right,
                    )
                    if step < 4 and half in ag_halves(step + 1, side):
                        ag_send(step + 1, side, half)
        for side in (0, 1):
            sib_send(step, side)

    def weights_complete():
        arrived(weight_part(0, 1 - c, None), sg_r.at[0], sibling)
        for step in range(1, 5):
            for side in (0, 1):
                index = 1 + 2 * (step - 1) + side
                part = weight_part(ag_shift(step, side), 1 - c, sib_half(step, side))
                arrived(part, sg_r.at[index], sibling)

    def hidden_terms(b):
        first, last = BATCHES[b]
        base = 0 if b == 0 else BATCHES[1][0]
        lanes = slice((first - base) * CAP, (last - base) * CAP)
        return (back_a, hid_a, lanes) if b == 0 else (back_b, hid_b, lanes)


    def batch(first, last, lo, lanes=slice(None)):
        part = rows[first:last, lo : lo + CAP, lanes]
        return part.reshape((last - first) * CAP, part.shape[2])

    def forward(b):
        first, last = BATCHES[b]
        pre = dot(weights[0 : 2 * HID, :], batch(first, last, 0), 1, 1)
        back_hidden = dot(weights[2 * HID : HID3, :], batch(first, last, CAP), 1, 1)
        pre_gate, pre_up = pre[0:HID], pre[HID : 2 * HID]
        s = jax.nn.sigmoid(pre_gate)
        active = pre_gate * s
        back_ref, hid_ref, lanes = hidden_terms(b)
        hid_ref[:, lanes] = (active * pre_up).astype(BF16)
        back_ref[0:HID, lanes] = (back_hidden * pre_up * s * (1.0 + pre_gate * (1.0 - s))).astype(BF16)
        back_ref[HID : 2 * HID, lanes] = (back_hidden * active).astype(BF16)

    def row_grads(b):
        first, last = BATCHES[b]
        back_ref, _, terms = hidden_terms(b)
        for q in range(4):
            lanes = slice(q * width, (q + 1) * width)
            part = dot(back_ref[:, terms], weights[0 : 2 * HID, lanes], 0, 0).astype(BF16)
            row_grad[first:last, :, lanes] = part.reshape(last - first, CAP, width)

    def rs_send(j):
        for index, (shift, device) in enumerate(((1, x_right), (3, x_left), (2, x_far))):
            send(
                row_grad.at[j, :, quarter(shift)], xs_in.at[j, index], xs_r.at[j, index], device,
            )

    def rs_finish(j):
        total = row_grad[j, :, quarter(0)].astype(F32)
        for index, device in enumerate((x_left, x_right, x_far)):
            arrived(xs_in.at[j, index], xs_r.at[j, index], device)
            total = total + xs_in[j, index].astype(F32)
        if j == 0:
            ret[0] = total.astype(BF16)
        else:
            yback[j] = total.astype(BF16)
            send(yback.at[j], ret.at[j], yb_r.at[j], at_y(8 - SHIFTS[j]))

    def half_quarter(shift, side):
        return pl.ds(pl.multiple_of(((m + shift) % 4) * width + side * (width // 2), width // 2), width // 2)

    def group_start(g):
        first, last = GROUPS[g]
        for side, device in enumerate((x_right, x_left)):
            send(
                row_grad.at[first:last, :, half_quarter(2, side)], gr_in.at[side, first:last],
                gs_r.at[g, side], device,
            )

    def group_pass(g):
        first, last = GROUPS[g]
        for side, (shift, device, source) in enumerate(((1, x_right, x_left), (3, x_left, x_right))):
            arrived(gr_in.at[side, first:last], gs_r.at[g, side], source)
            lanes = half_quarter(shift, side)
            for j in range(first, last):
                total = row_grad[j, :, lanes].astype(F32) + gr_in[side, j].astype(F32)
                row_grad[j, :, lanes] = total.astype(BF16)
            send(
                row_grad.at[first:last, :, quarter(shift)], gx_in.at[side, first:last],
                gs_r.at[g, 2 + side], device,
            )

    def group_finish(g):
        first, last = GROUPS[g]
        for side, source in enumerate((x_left, x_right)):
            arrived(gx_in.at[side, first:last], gs_r.at[g, 2 + side], source)
        for j in range(first, last):
            total = row_grad[j, :, quarter(0)].astype(F32) + gx_in[0, j].astype(F32) + gx_in[1, j].astype(F32)
            yback[j] = total.astype(BF16)
            send(yback.at[j], ret.at[j], yb_r.at[j], at_y(8 - SHIFTS[j]))

    def weight_early():
        first, last = BATCHES[0]
        for k in range(8):
            lanes = slice(256 * k, 256 * (k + 1))
            wacc[0 : 2 * HID, lanes] = dot(back_a[...], batch(first, last, 0, lanes), 1, 0)
            wacc[2 * HID : HID3, lanes] = dot(hid_a[...], batch(first, last, CAP, lanes), 1, 0)

    def weight_chunk(index):
        shift = chunk_shifts[index]
        first, last = BATCHES[1][0], SLOTS
        lanes = pl.ds(pl.multiple_of(((z + shift) % 8) * 256, 256), 256)
        grad_gu = wacc[0 : 2 * HID, lanes] + dot(back_b[...], batch(first, last, 0, lanes), 1, 0)
        grad_d = wacc[2 * HID : HID3, lanes] + dot(hid_b[...], batch(first, last, CAP, lanes), 1, 0)
        wgrad[0 : 2 * HID, lanes] = grad_gu.astype(BF16)
        wgrad[2 * HID : HID3, lanes] = grad_d.astype(BF16)
        send(wgrad.at[:, block(shift, 1 - c)], sib_rs.at[index], sr_r.at[index], sibling)

    chunk_shifts = (4, 3, 5, 2, 6, 1, 7, 0)

    def pair_ready(index):
        arrived(sib_rs.at[index], sr_r.at[index], sibling)

    def pair_sum(index, lo, size):
        mine = wgrad[pl.ds(lo, size), block(chunk_shifts[index], c)].astype(F32)
        return mine + sib_rs[index, pl.ds(lo, size), :].astype(F32)

    def ring_part(ref, side, step, piece):
        return ref.at[side, step - 1, pl.ds(*PIECES[piece])]

    def ring_send(side, step, piece, total):
        lo, size = PIECES[piece]
        ring_out[side, step - 1, pl.ds(lo, size), :] = total.astype(BF16)
        send(
            ring_part(ring_out, side, step, piece), ring_part(ring_in, side, step, piece),
            rr_r.at[side, step - 1, piece], (z_right, z_left)[side],
        )

    def ring_recv(side, step, piece):
        lo, size = PIECES[piece]
        arrived(
            ring_part(ring_in, side, step, piece), rr_r.at[side, step - 1, piece],
            (z_left, z_right)[side],
        )
        return ring_in[side, step - 1, pl.ds(lo, size), :].astype(F32)

    def ring_first():
        pair_ready(0)
        for turn in (0, 1):
            for side in (0, 1):
                piece = 2 * side + turn
                ring_send(side, 1, piece, pair_sum(0, *PIECES[piece]))

    paired = set()

    def ring_step(step, half):
        if step not in paired:
            paired.add(step)
            for side in (0, 1):
                pair_ready(2 * step - 3 + side)
        for turn in (2 * half, 2 * half + 1):
            for side in (0, 1):
                piece = (turn + 2 * side) % 4
                total = pair_sum(2 * step - 3 + side, *PIECES[piece])
                if step > 2 or piece // 2 == side:
                    total = total + ring_recv(side, step - 1, piece)
                ring_send(side, step, piece, total)

    def weight_outputs():
        pair_ready(7)
        outs = ((0, HID, gate_out), (HID, 2 * HID, up_out), (2 * HID, HID3, down_out))
        for piece in range(4):
            lo, size = PIECES[piece]
            total = pair_sum(7, lo, size) + ring_recv(0, 4, piece) + ring_recv(1, 4, piece)
            for first, last, out in outs:
                start, stop = max(first, lo), min(last, lo + size)
                if start < stop:
                    out[0, start - first : stop - first] = total[start - lo : stop - lo]

    def token_outputs():
        for j in range(1, SLOTS):
            arrived(ret.at[j], yb_r.at[j], at_y(SHIFTS[j]))
        back_rows = ret[...].reshape(SLOTS * CAP, width)
        tok_out[...] = dot(pack[...], back_rows, 0, 0).astype(BF16)

    def pack_full():
        loads[7].wait()
        loads[8].wait()
        for j, part, grad_part in packed(0, 1, tokf, gradf):
            rows[0, 0:CAP, :] = part
            rows[0, CAP : 2 * CAP, :] = grad_part
        for j, part, grad_part in packed(FAR, SLOTS, tokf, gradf):
            sendf[j - FAR, 0:CAP, :] = part
            sendf[j - FAR, CAP : 2 * CAP, :] = grad_part

    def pack_quarter(lo, hi):
        for j, part, grad_part in packed(lo, hi, tokq, gradq):
            sendq[j - 1, 0:CAP, :] = part
            sendq[j - 1, CAP : 2 * CAP, :] = grad_part

    loads[2].wait()
    loads[3].wait()
    pack_quarter(1, 3)
    pl.semaphore_wait(barrier, len(partners))

    y_send(2, 1, grad_rows)
    y_send(1, 1, grad_rows)
    ag_start()
    pack_quarter(3, FAR)
    y_send(2, 0, token_rows)
    y_send(1, 0, token_rows)
    y_send(3, 1, grad_rows)
    y_send(4, 1, grad_rows)
    ag_step(1)
    y_send(3, 0, token_rows)
    y_arrived(1, 1, grad_rows)
    x_send(1, 1, grad_rows)
    pack_full()
    y_arrived(2, 1, grad_rows)
    x_send(2, 1, grad_rows)
    y_send(4, 0, token_rows)
    y_arrived(1, 0, token_rows)
    x_send(1, 0, token_rows)
    y_arrived(2, 0, token_rows)
    x_send(2, 0, token_rows)
    ag_step(2)
    y_arrived(4, 1, grad_rows)
    x_send(4, 1, grad_rows)
    y_send(5)
    y_arrived(3, 1, grad_rows)
    x_send(3, 1, grad_rows)
    x_forward(1, 0)
    x_forward(1, 1)
    y_arrived(4, 0, token_rows)
    x_send(4, 0, token_rows)
    y_arrived(3, 0, token_rows)
    x_send(3, 0, token_rows)
    y_send(7)
    ag_step(3)
    y_send(6)
    x_forward(2, 1)
    x_forward(2, 0)
    x_forward(3, 1)
    x_forward(4, 1)
    x_forward(4, 0)
    x_complete(1)
    x_forward(3, 0)
    y_arrived(5)
    x_send(5)
    x_complete(2)
    ag_step(4)
    weights_complete()
    x_complete(4)
    forward(0)
    x_complete(3)
    forward(1)
    row_grads(1)
    group_start(1)
    weight_early()
    row_grads(0)
    group_start(0)
    y_arrived(7)
    y_arrived(6)
    x_complete(5)
    forward(2)
    row_grads(2)
    rs_send(5)
    weight_chunk(0)
    weight_chunk(1)
    weight_chunk(2)
    weight_chunk(3)
    group_pass(0)
    ring_first()
    weight_chunk(4)
    weight_chunk(5)
    ring_step(2, 1)
    group_pass(1)
    rs_send(6)
    rs_send(7)
    ring_step(2, 0)
    rs_finish(5)
    ring_step(3, 1)
    group_finish(0)
    ring_step(3, 0)
    weight_chunk(6)
    group_finish(1)
    rs_send(0)
    ring_step(4, 1)
    ring_step(4, 0)
    weight_chunk(7)
    rs_finish(6)
    rs_finish(7)
    rs_finish(0)
    drain(24)
    weight_outputs()
    drain(0)
    token_outputs()

    drain(0)


def finish(tok_ref, gate_ref, up_ref, down_ref, tok_out, gate_out, up_out, down_out):
    tok_out[...] = tok_ref[...]
    gate_out[...] = gate_ref[...]
    up_out[...] = up_ref[...]
    down_out[...] = down_ref[...]


def on_device(tokens, out_grad, routes, gate_values, gate_proj, up_proj, down_proj):
    count, model = tokens.shape
    width = model // lax.axis_size("mp")
    sems = pltpu.SemaphoreType.DMA
    early = BATCHES[0][1]
    vmem = pl.BlockSpec(memory_space=pltpu.VMEM)
    hbm = pl.BlockSpec(memory_space=pltpu.HBM)
    weight_out = jax.ShapeDtypeStruct(gate_proj.shape, F32)
    results = pl.pallas_call(
        kernel,
        out_shape=(jax.ShapeDtypeStruct((count, width), BF16), weight_out, weight_out, weight_out),
        in_specs=[hbm] * 7,
        out_specs=(vmem, vmem, vmem, vmem),
        scratch_shapes=[
            pltpu.VMEM((count, width), BF16),
            pltpu.VMEM((count, width), BF16),
            pltpu.VMEM((count, model), BF16),
            pltpu.VMEM((count, model), BF16),
            pltpu.VMEM((2, count), jnp.int32),
            pltpu.VMEM((2, count), F32),
            pltpu.VMEM((SLOTS * CAP, count), BF16),
            pltpu.VMEM((FAR - 1, 2 * CAP, width), BF16),
            pltpu.VMEM((len(NEAR), 2 * CAP, model), BF16),
            pltpu.VMEM((SLOTS, 2 * CAP, model), BF16),
            pltpu.VMEM((HID3, model), BF16),
            pltpu.VMEM((2 * HID, early * CAP), BF16),
            pltpu.VMEM((2 * HID, (SLOTS - early) * CAP), BF16),
            pltpu.VMEM((HID, early * CAP), BF16),
            pltpu.VMEM((HID, (SLOTS - early) * CAP), BF16),
            pltpu.VMEM((SLOTS, CAP, model), BF16),
            pltpu.VMEM((HID3, model), F32),
            pltpu.VMEM((HID3, model), BF16),
            pltpu.VMEM((8, HID3, 128), BF16),
            pltpu.VMEM((2, 4, HID3, 128), BF16),
            pltpu.VMEM((2, 4, HID3, 128), BF16),
            pltpu.VMEM((SLOTS, 3, CAP, width), BF16),
            pltpu.VMEM((2, SLOTS, CAP, width // 2), BF16),
            pltpu.VMEM((2, SLOTS, CAP, width), BF16),
            pltpu.VMEM((SLOTS, CAP, width), BF16),
            pltpu.VMEM((SLOTS, CAP, width), BF16),
            sems((9,)),
            sems((SENDS,)),
            sems((RECVS,)),
        ],
        compiler_params=pltpu.CompilerParams(
            collective_id=0, has_side_effects=True, vmem_limit_bytes=56 * 1024 * 1024
        ),
        cost_estimate=pl.CostEstimate(flops=2300000000, bytes_accessed=4000000, transcendentals=70000),
        name="experts",
    )(tokens, out_grad, routes.T, gate_values.T, gate_proj, up_proj, down_proj)
    return pl.pallas_call(
        finish,
        out_shape=tuple(jax.ShapeDtypeStruct(result.shape, result.dtype) for result in results),
        in_specs=[vmem] * 4,
        out_specs=(vmem,) * 4,
        name="finish",
    )(*results)


def solution(mesh):
    tokens_in = P(("dp", "expert"), None)
    weights_in = P("expert", "mp", "dp")
    return jax.shard_map(
        on_device,
        mesh=mesh,
        in_specs=(tokens_in, tokens_in, tokens_in, tokens_in, weights_in, weights_in, weights_in),
        out_specs=(P(("dp", "expert"), "mp"), weights_in, weights_in, weights_in),
        check_vma=False,
    )
```

```python
import functools

import jax
import jax.numpy as jnp
from jax import lax
from jax.experimental import pallas as pl
from jax.experimental.pallas import tpu as pltpu
from jax.sharding import PartitionSpec as P

MESH = pl.DeviceIdType.MESH
F32 = jnp.float32
BF16 = jnp.bfloat16

SHIFTS = (0, 2, 6, 3, 5, 4, 1, 7)
SLOTS = 8
FAR = 6
NEAR = (6, 7)
SPLIT = (1, 2, 3, 4)
LAST_FAR = 5
BATCHES = ((0, 3), (3, 5), (5, 8))
GROUPS = ((1, 3), (3, 5))
CAP = 48
HID = 176
HID3 = 3 * HID
HALVES = ((0, 272), (272, 256))
PIECES = HALVES


SENDS = 24
RECVS = 69

PART = len(PIECES) // 2


class Numbered:
    def __init__(self, sems, table, kind):
        self.sems, self.table, self.kind = sems, table, kind

    @property
    def at(self):
        return self

    def __getitem__(self, key):
        return self.sems.at[self.table.setdefault((self.kind, key), len(self.table))]


def dot(a, b, ca, cb):
    return lax.dot_general(a, b, (((ca,), (cb,)), ((), ())), preferred_element_type=F32)


def kernel(
    tok_hbm, grad_hbm, routes_hbm, gates_hbm, gate_hbm, up_hbm, down_hbm,
    tok_out, gate_out, up_out, down_out,
    tokq, gradq, tokf, gradf, routes_ref, gates_ref, pack, sendq, sendf, rows, weights, back_a, back_b, hid_a, hid_b,
    row_grad, wacc, wgrad, sib_rs, ring_in, ring_out, xs_in, gr_in, gx_in, yback, ret,
    loc, send_sems, recv_sems,
):
    table = {}
    kinds = [Numbered(recv_sems, table, kind) for kind in range(9)]
    y_r, x_r, ag_r, sg_r, xs_r, gs_r, yb_r, sr_r, rr_r = kinds
    d, e, m = lax.axis_index("dp"), lax.axis_index("expert"), lax.axis_index("mp")
    z, c = d // 2, d % 2
    width = tokq.shape[1]

    def at_z(shift, core=None):
        return ((((z + shift) % 8) * 2 + (c if core is None else core)), e, m)

    def at_y(shift):
        return (d, (e + shift) % 8, m)

    def at_x(shift):
        return (d, e, (m + shift) % 4)

    z_right, z_left, sibling = at_z(1), at_z(7), at_z(0, 1 - c)
    x_right, x_left, x_far = at_x(1), at_x(3), at_x(2)

    def quarter(shift):
        return pl.ds(pl.multiple_of(((m + shift) % 4) * width, width), width)

    def block(shift, core):
        return pl.ds(pl.multiple_of((((z + shift) % 8) * 2 + core) * 128, 128), 128)

    def remote(src, dst, send, recv, device):
        return pltpu.make_async_remote_copy(
            src_ref=src, dst_ref=dst, send_sem=send, recv_sem=recv, device_id=device, device_id_type=MESH
        )

    pending, free = [], list(range(SENDS))

    def drain(newest):
        while len(pending) > newest:
            copy, index = pending.pop(0)
            copy.wait_send()
            free.append(index)

    def send(src, dst, recv_sem, device):
        if not free:
            drain(SENDS - 1)
        index = free.pop(0)
        copy = remote(src, dst, send_sems.at[index], recv_sem, device)
        copy.start()
        pending.append((copy, index))

    def arrived(dst, recv_sem, device):
        remote(dst, dst, send_sems.at[0], recv_sem, device).wait_recv()

    barrier = pltpu.get_barrier_semaphore()
    partners = [z_right, z_left, sibling, x_right, x_left, x_far] + [at_y(k) for k in range(1, 8)]
    for partner in partners:
        pl.semaphore_signal(barrier, inc=1, device_id=partner, device_id_type=MESH)

    own = block(0, c)
    loads = [
        pltpu.make_async_copy(routes_hbm, routes_ref, loc.at[0]),
        pltpu.make_async_copy(gates_hbm, gates_ref, loc.at[1]),
        pltpu.make_async_copy(tok_hbm.at[:, quarter(0)], tokq, loc.at[2]),
        pltpu.make_async_copy(grad_hbm.at[:, quarter(0)], gradq, loc.at[3]),
        pltpu.make_async_copy(gate_hbm.at[0], weights.at[pl.ds(0, HID), own], loc.at[4]),
        pltpu.make_async_copy(up_hbm.at[0], weights.at[pl.ds(HID, HID), own], loc.at[5]),
        pltpu.make_async_copy(down_hbm.at[0], weights.at[pl.ds(2 * HID, HID), own], loc.at[6]),
        pltpu.make_async_copy(tok_hbm, tokf, loc.at[7]),
        pltpu.make_async_copy(grad_hbm, gradf, loc.at[8]),
    ]
    for copy in loads:
        copy.start()

    loads[0].wait()
    loads[1].wait()
    count = tokq.shape[0]
    slot_id = lax.broadcasted_iota(jnp.int32, (SLOTS, count), 0)
    wanted = jnp.zeros((SLOTS, count), jnp.int32)
    for j, shift in enumerate(SHIFTS):
        wanted = jnp.where(slot_id == j, (e + shift) % 8, wanted)
    first = routes_ref[0:1, :] == wanted
    second = routes_ref[1:2, :] == wanted
    named = jnp.where(first, 1.0, jnp.where(second, 1.0, 0.0))
    value = jnp.where(first, gates_ref[0:1, :], jnp.where(second, gates_ref[1:2, :], 0.0))
    earlier = jnp.where(
        lax.broadcasted_iota(jnp.int32, (count, count), 0) < lax.broadcasted_iota(jnp.int32, (count, count), 1),
        1.0, 0.0,
    ).astype(BF16)
    rank = dot(named.astype(BF16), earlier, 1, 0).astype(jnp.int32)
    place = jnp.where(named > 0.5, rank, -1)
    row_id = lax.broadcasted_iota(jnp.int32, (CAP, count), 0)
    scales = []
    for j in range(SLOTS):
        taken = place[j : j + 1, :] == row_id
        pack[pl.ds(j * CAP, CAP), :] = jnp.where(taken, 1.0, 0.0).astype(BF16)
        scales.append(jnp.sum(jnp.where(taken, value[j : j + 1, :], 0.0), axis=1, keepdims=True))

    def packed(lo, hi, tok, grad):
        chosen = pack[pl.ds(lo * CAP, (hi - lo) * CAP), :]
        taken_rows = dot(chosen, tok[...], 1, 0).astype(BF16)
        taken_grads = dot(chosen, grad[...], 1, 0)
        for j in range(lo, hi):
            part = slice((j - lo) * CAP, (j - lo + 1) * CAP)
            yield j, taken_rows[part], (taken_grads[part] * scales[j]).astype(BF16)

    both, token_rows, grad_rows = pl.ds(0, 2 * CAP), pl.ds(0, CAP), pl.ds(CAP, CAP)

    def y_send(j, part=0, span=both):
        if j in NEAR:
            send(sendf.at[j - FAR], rows.at[j], y_r.at[j, 0], at_y(SHIFTS[j]))
        else:
            send(
                sendq.at[j - 1, span], rows.at[j, span, quarter(0)], y_r.at[j, part], at_y(SHIFTS[j]),
            )

    def y_arrived(j, part=0, span=both):
        where = rows.at[j] if j in NEAR else rows.at[j, span, quarter(0)]
        arrived(where, y_r.at[j, part], at_y(8 - SHIFTS[j]))

    def x_sem(j, part, side):
        late = j == LAST_FAR or side != part
        return x_r.at[j - 1, 2 if late else part]

    def x_send(j, part=0, span=both):
        block_out = rows.at[j, span, quarter(0)]
        send(block_out, block_out, x_sem(j, part, 0), x_right)
        send(block_out, block_out, x_sem(j, part, 1), x_left)
        if j == LAST_FAR:
            send(block_out, block_out, x_sem(j, part, 2), x_far)

    def x_arrived(j, side, part=0, span=both):
        shift, device = ((3, x_left), (1, x_right), (2, x_far))[side]
        arrived(rows.at[j, span, quarter(shift)], x_sem(j, part, side), device)

    def forward_send(j, side):
        block_out = rows.at[j, grad_rows if side else token_rows, quarter(1 if side else 3)]
        device = x_left if side else x_right
        send(block_out, block_out, x_sem(j, side, 2), device)

    def x_forward(j, side):
        x_arrived(j, side, side, (token_rows, grad_rows)[side])
        forward_send(j, side)

    def x_complete(j):
        span = pl.ds(0, (3 if j == LAST_FAR else 2) * width)
        arrived(rows.at[j, :, span], x_sem(j, 0, 2), x_left)

    def weight_part(shift, core, half):
        if half is None:
            return weights.at[:, block(shift, core)]
        return weights.at[pl.ds(*HALVES[half]), block(shift, core)]

    def ag_shift(step, side):
        return (8 - step) % 8 if side == 0 else step

    def ag_halves(step, side):
        return (side,) if step == 4 else (0, 1)

    def ag_send(step, side, half):
        part = weight_part(ag_shift(step - 1, side), c, half)
        device = z_right if side == 0 else z_left
        send(part, part, ag_r.at[side, step - 1, half], device)

    def sib_half(step, side):
        return side if step == 4 else None

    def sib_send(step, side):
        part = weight_part(ag_shift(step, side), c, sib_half(step, side))
        send(part, part, sg_r.at[0], sibling)

    def ag_start():
        for copy in loads[4:7]:
            copy.wait()
        for half in (0, 1):
            for side in (0, 1):
                ag_send(1, side, half)
        sib_send(0, 0)

    def ag_step(step):
        for half in (0, 1):
            for side in (0, 1):
                if half in ag_halves(step, side):
                    arrived(
                        weight_part(ag_shift(step, side), c, half), ag_r.at[side, step - 1, half], z_left if side == 0 else z_right,
                    )
                    if step < 4 and half in ag_halves(step + 1, side):
                        ag_send(step + 1, side, half)
        for side in (0, 1):
            sib_send(step, side)

    def weights_complete():
        arrived(weights.at[:, pl.ds(0, weights.shape[1] // 2)], sg_r.at[0], sibling)

    def hidden_terms(b):
        first, last = BATCHES[b]
        base = 0 if b == 0 else BATCHES[1][0]
        lanes = slice((first - base) * CAP, (last - base) * CAP)
        return (back_a, hid_a, lanes) if b == 0 else (back_b, hid_b, lanes)


    def batch(first, last, lo, lanes=slice(None)):
        part = rows[first:last, lo : lo + CAP, lanes]
        return part.reshape((last - first) * CAP, part.shape[2])

    def forward(b):
        first, last = BATCHES[b]
        pre = dot(weights[0 : 2 * HID, :], batch(first, last, 0), 1, 1)
        back_hidden = dot(weights[2 * HID : HID3, :], batch(first, last, CAP), 1, 1)
        pre_gate, pre_up = pre[0:HID], pre[HID : 2 * HID]
        s = jax.nn.sigmoid(pre_gate)
        active = pre_gate * s
        back_ref, hid_ref, lanes = hidden_terms(b)
        hid_ref[:, lanes] = (active * pre_up).astype(BF16)
        back_ref[0:HID, lanes] = (back_hidden * pre_up * s * (1.0 + pre_gate * (1.0 - s))).astype(BF16)
        back_ref[HID : 2 * HID, lanes] = (back_hidden * active).astype(BF16)

    def row_grads(b):
        first, last = BATCHES[b]
        back_ref, _, terms = hidden_terms(b)
        for q in range(4):
            lanes = slice(q * width, (q + 1) * width)
            part = dot(back_ref[:, terms], weights[0 : 2 * HID, lanes], 0, 0).astype(BF16)
            row_grad[first:last, :, lanes] = part.reshape(last - first, CAP, width)

    def rs_send(j):
        for index, (shift, device) in enumerate(((1, x_right), (3, x_left), (2, x_far))):
            send(
                row_grad.at[j, :, quarter(shift)], xs_in.at[j, index], xs_r.at[j], device,
            )

    def rs_finish(j):
        arrived(xs_in.at[j], xs_r.at[j], x_far)
        total = row_grad[j, :, quarter(0)].astype(F32)
        for index in range(3):
            total = total + xs_in[j, index].astype(F32)
        if j == 0:
            ret[0] = total.astype(BF16)
        else:
            yback[j] = total.astype(BF16)
            send(yback.at[j], ret.at[j], yb_r.at[0], at_y(8 - SHIFTS[j]))

    def half_quarter(shift, side):
        return pl.ds(pl.multiple_of(((m + shift) % 4) * width + side * (width // 2), width // 2), width // 2)

    def group_start(g):
        first, last = GROUPS[g]
        for side, device in enumerate((x_right, x_left)):
            send(
                row_grad.at[first:last, :, half_quarter(2, side)], gr_in.at[side, first:last],
                gs_r.at[g, side], device,
            )

    def group_pass(g):
        first, last = GROUPS[g]
        for side, (shift, device, source) in enumerate(((1, x_right, x_left), (3, x_left, x_right))):
            arrived(gr_in.at[side, first:last], gs_r.at[g, side], source)
            lanes = half_quarter(shift, side)
            for j in range(first, last):
                total = row_grad[j, :, lanes].astype(F32) + gr_in[side, j].astype(F32)
                row_grad[j, :, lanes] = total.astype(BF16)
            send(
                row_grad.at[first:last, :, quarter(shift)], gx_in.at[side, first:last],
                gs_r.at[g, 2], device,
            )

    def group_finish(g):
        first, last = GROUPS[g]
        arrived(gx_in.at[:, first:last], gs_r.at[g, 2], x_left)
        for j in range(first, last):
            total = row_grad[j, :, quarter(0)].astype(F32) + gx_in[0, j].astype(F32) + gx_in[1, j].astype(F32)
            yback[j] = total.astype(BF16)
            send(yback.at[j], ret.at[j], yb_r.at[0], at_y(8 - SHIFTS[j]))

    def weight_early():
        first, last = BATCHES[0]
        for k in range(8):
            lanes = slice(256 * k, 256 * (k + 1))
            wacc[0 : 2 * HID, lanes] = dot(back_a[...], batch(first, last, 0, lanes), 1, 0)
            wacc[2 * HID : HID3, lanes] = dot(hid_a[...], batch(first, last, CAP, lanes), 1, 0)

    def weight_chunk(index):
        shift = chunk_shifts[index]
        first, last = BATCHES[1][0], SLOTS
        lanes = pl.ds(pl.multiple_of(((z + shift) % 8) * 256, 256), 256)
        grad_gu = wacc[0 : 2 * HID, lanes] + dot(back_b[...], batch(first, last, 0, lanes), 1, 0)
        grad_d = wacc[2 * HID : HID3, lanes] + dot(hid_b[...], batch(first, last, CAP, lanes), 1, 0)
        wgrad[0 : 2 * HID, lanes] = grad_gu.astype(BF16)
        wgrad[2 * HID : HID3, lanes] = grad_d.astype(BF16)
        send(wgrad.at[:, block(shift, 1 - c)], sib_rs.at[index], sr_r.at[(index + 1) // 2], sibling)

    chunk_shifts = (4, 3, 5, 2, 6, 1, 7, 0)

    def pair_ready(index):
        arrived(sib_rs.at[index], sr_r.at[(index + 1) // 2], sibling)

    def pair_sum(index, lo, size):
        mine = wgrad[pl.ds(lo, size), block(chunk_shifts[index], c)].astype(F32)
        return mine + sib_rs[index, pl.ds(lo, size), :].astype(F32)

    def ring_part(ref, side, step, piece):
        return ref.at[side, step - 1, pl.ds(*PIECES[piece])]

    def ring_send(side, step, piece, total):
        lo, size = PIECES[piece]
        ring_out[side, step - 1, pl.ds(lo, size), :] = total.astype(BF16)
        send(
            ring_part(ring_out, side, step, piece), ring_part(ring_in, side, step, piece),
            rr_r.at[side, step - 1, piece], (z_right, z_left)[side],
        )

    def ring_recv(side, step, piece):
        lo, size = PIECES[piece]
        arrived(
            ring_part(ring_in, side, step, piece), rr_r.at[side, step - 1, piece],
            (z_left, z_right)[side],
        )
        return ring_in[side, step - 1, pl.ds(lo, size), :].astype(F32)

    def ring_first():
        pair_ready(0)
        for turn in range(PART):
            for side in (0, 1):
                piece = PART * side + turn
                ring_send(side, 1, piece, pair_sum(0, *PIECES[piece]))

    paired = set()

    def ring_step(step, half):
        if step not in paired:
            paired.add(step)
            arrived(sib_rs.at[2 * step - 3 : 2 * step - 1], sr_r.at[step - 1], sibling)
        for turn in range(PART * half, PART * (half + 1)):
            for side in (0, 1):
                piece = (turn + PART * side) % len(PIECES)
                total = pair_sum(2 * step - 3 + side, *PIECES[piece])
                if step > 2 or piece // PART == side:
                    total = total + ring_recv(side, step - 1, piece)
                ring_send(side, step, piece, total)

    def weight_outputs():
        pair_ready(7)
        outs = ((0, HID, gate_out), (HID, 2 * HID, up_out), (2 * HID, HID3, down_out))
        for piece in range(len(PIECES)):
            lo, size = PIECES[piece]
            total = pair_sum(7, lo, size) + ring_recv(0, 4, piece) + ring_recv(1, 4, piece)
            for first, last, out in outs:
                start, stop = max(first, lo), min(last, lo + size)
                if start < stop:
                    out[0, start - first : stop - first] = total[start - lo : stop - lo]

    def token_outputs():
        arrived(ret.at[1:SLOTS], yb_r.at[0], at_y(1))
        back_rows = ret[...].reshape(SLOTS * CAP, width)
        tok_out[...] = dot(pack[...], back_rows, 0, 0).astype(BF16)

    def pack_full():
        loads[7].wait()
        loads[8].wait()
        for j, part, grad_part in packed(0, 1, tokf, gradf):
            rows[0, 0:CAP, :] = part
            rows[0, CAP : 2 * CAP, :] = grad_part
        for j, part, grad_part in packed(FAR, SLOTS, tokf, gradf):
            sendf[j - FAR, 0:CAP, :] = part
            sendf[j - FAR, CAP : 2 * CAP, :] = grad_part

    def pack_quarter(lo, hi):
        for j, part, grad_part in packed(lo, hi, tokq, gradq):
            sendq[j - 1, 0:CAP, :] = part
            sendq[j - 1, CAP : 2 * CAP, :] = grad_part

    loads[2].wait()
    loads[3].wait()
    pack_quarter(1, 3)
    pl.semaphore_wait(barrier, len(partners))

    y_send(2, 1, grad_rows)
    y_send(1, 1, grad_rows)
    ag_start()
    pack_quarter(3, FAR)
    y_send(2, 0, token_rows)
    y_send(1, 0, token_rows)
    y_send(3, 1, grad_rows)
    y_send(4, 1, grad_rows)
    ag_step(1)
    y_send(3, 0, token_rows)
    y_arrived(1, 1, grad_rows)
    x_send(1, 1, grad_rows)
    pack_full()
    y_arrived(2, 1, grad_rows)
    x_send(2, 1, grad_rows)
    y_send(4, 0, token_rows)
    y_arrived(1, 0, token_rows)
    x_send(1, 0, token_rows)
    y_arrived(2, 0, token_rows)
    x_send(2, 0, token_rows)
    ag_step(2)
    y_arrived(4, 1, grad_rows)
    x_send(4, 1, grad_rows)
    y_send(5)
    y_arrived(3, 1, grad_rows)
    x_send(3, 1, grad_rows)
    x_forward(1, 0)
    x_forward(1, 1)
    y_arrived(4, 0, token_rows)
    x_send(4, 0, token_rows)
    y_arrived(3, 0, token_rows)
    x_send(3, 0, token_rows)
    y_send(7)
    ag_step(3)
    y_send(6)
    x_forward(2, 1)
    x_forward(2, 0)
    x_forward(3, 1)
    x_forward(4, 1)
    x_forward(4, 0)
    x_complete(1)
    x_forward(3, 0)
    y_arrived(5)
    x_send(5)
    x_complete(2)
    ag_step(4)
    weights_complete()
    x_complete(4)
    forward(0)
    x_complete(3)
    forward(1)
    row_grads(1)
    group_start(1)
    weight_early()
    row_grads(0)
    group_start(0)
    y_arrived(7)
    y_arrived(6)
    x_complete(5)
    forward(2)
    row_grads(2)
    rs_send(5)
    weight_chunk(0)
    weight_chunk(1)
    weight_chunk(2)
    weight_chunk(3)
    group_pass(0)
    ring_first()
    weight_chunk(4)
    weight_chunk(5)
    ring_step(2, 1)
    group_pass(1)
    rs_send(6)
    rs_send(7)
    ring_step(2, 0)
    rs_finish(5)
    ring_step(3, 1)
    group_finish(0)
    ring_step(3, 0)
    weight_chunk(6)
    group_finish(1)
    rs_send(0)
    ring_step(4, 1)
    ring_step(4, 0)
    weight_chunk(7)
    rs_finish(6)
    rs_finish(7)
    rs_finish(0)
    drain(24)
    weight_outputs()
    drain(0)
    token_outputs()

    drain(0)


def finish(tok_ref, gate_ref, up_ref, down_ref, tok_out, gate_out, up_out, down_out):
    tok_out[...] = tok_ref[...]
    gate_out[...] = gate_ref[...]
    up_out[...] = up_ref[...]
    down_out[...] = down_ref[...]


def on_device(tokens, out_grad, routes, gate_values, gate_proj, up_proj, down_proj):
    count, model = tokens.shape
    width = model // lax.axis_size("mp")
    sems = pltpu.SemaphoreType.DMA
    early = BATCHES[0][1]
    vmem = pl.BlockSpec(memory_space=pltpu.VMEM)
    hbm = pl.BlockSpec(memory_space=pltpu.HBM)
    weight_out = jax.ShapeDtypeStruct(gate_proj.shape, F32)
    results = pl.pallas_call(
        kernel,
        out_shape=(jax.ShapeDtypeStruct((count, width), BF16), weight_out, weight_out, weight_out),
        in_specs=[hbm] * 7,
        out_specs=(vmem, vmem, vmem, vmem),
        scratch_shapes=[
            pltpu.VMEM((count, width), BF16),
            pltpu.VMEM((count, width), BF16),
            pltpu.VMEM((count, model), BF16),
            pltpu.VMEM((count, model), BF16),
            pltpu.VMEM((2, count), jnp.int32),
            pltpu.VMEM((2, count), F32),
            pltpu.VMEM((SLOTS * CAP, count), BF16),
            pltpu.VMEM((FAR - 1, 2 * CAP, width), BF16),
            pltpu.VMEM((len(NEAR), 2 * CAP, model), BF16),
            pltpu.VMEM((SLOTS, 2 * CAP, model), BF16),
            pltpu.VMEM((HID3, model), BF16),
            pltpu.VMEM((2 * HID, early * CAP), BF16),
            pltpu.VMEM((2 * HID, (SLOTS - early) * CAP), BF16),
            pltpu.VMEM((HID, early * CAP), BF16),
            pltpu.VMEM((HID, (SLOTS - early) * CAP), BF16),
            pltpu.VMEM((SLOTS, CAP, model), BF16),
            pltpu.VMEM((HID3, model), F32),
            pltpu.VMEM((HID3, model), BF16),
            pltpu.VMEM((8, HID3, 128), BF16),
            pltpu.VMEM((2, 4, HID3, 128), BF16),
            pltpu.VMEM((2, 4, HID3, 128), BF16),
            pltpu.VMEM((SLOTS, 3, CAP, width), BF16),
            pltpu.VMEM((2, SLOTS, CAP, width // 2), BF16),
            pltpu.VMEM((2, SLOTS, CAP, width), BF16),
            pltpu.VMEM((SLOTS, CAP, width), BF16),
            pltpu.VMEM((SLOTS, CAP, width), BF16),
            sems((9,)),
            sems((SENDS,)),
            sems((RECVS,)),
        ],
        compiler_params=pltpu.CompilerParams(
            collective_id=0, has_side_effects=True, vmem_limit_bytes=56 * 1024 * 1024
        ),
        cost_estimate=pl.CostEstimate(flops=2300000000, bytes_accessed=4000000, transcendentals=70000),
        name="experts",
    )(tokens, out_grad, routes.T, gate_values.T, gate_proj, up_proj, down_proj)
    return pl.pallas_call(
        finish,
        out_shape=tuple(jax.ShapeDtypeStruct(result.shape, result.dtype) for result in results),
        in_specs=[vmem] * 4,
        out_specs=(vmem,) * 4,
        name="finish",
    )(*results)


def solution(mesh):
    tokens_in = P(("dp", "expert"), None)
    weights_in = P("expert", "mp", "dp")
    return jax.shard_map(
        on_device,
        mesh=mesh,
        in_specs=(tokens_in, tokens_in, tokens_in, tokens_in, weights_in, weights_in, weights_in),
        out_specs=(P(("dp", "expert"), "mp"), weights_in, weights_in, weights_in),
        check_vma=False,
    )
```
